256 devices in a mesh: dom: 64 (over z, x, y_lo), band: 4 (over y_hi, core).
Axes of the slice: x: 4, y: 4 (y_hi: 2, y_lo: 2; y = y_hi * 2 + y_lo), z: 8, core: 2. Of those that a mesh axis runs over, the one named last changes fastest.
Arguments:
- orbitals: float32 [128, 512, 8, 128], P('band', 'dom'), may hold values from -6 to 6
- potential: float32 [512, 8, 128], P('dom'), may hold values from -1 to 1
- slot_atom: int32 [1024], P('dom'), may hold values from -1 to 23, as said below
- point_offset: int32 [1024, 256], P('dom'), may hold values from 0 to 8191
- projector: float32 [1024, 4, 256], P('dom'), may hold values from -0.3125 to 0.3125
- coupling: float32 [4], replicated, may hold values from 0.5 to 2
Outputs:
- filtered: float32 [128, 512, 8, 128], P('band', 'dom')
- subspace_hamiltonian: float32 [128, 128], P(None, 'band')
- subspace_margin: float32 [128, 128], P(None, 'band')
The draws below stay inside these ranges and needn't reach their ends.
Inputs may be any that keep to these rules, and one draw needn't show every extreme that they name: `slot_atom`: entries of one slab's list rows are distinct where not -1. `point_offset`: cell indices inside the slab's own block.
All inputs are finite; a program needn't handle non-finite values.
Results may differ from the reference program's by a relative error of at most 0.0001.
Values sent between devices are 32-bit elements; how exact they have to be, the bound alone decides.
No kernel may reach another device: no remote copies, remote signals or barrier semaphores. Data moves between devices by JAX's collectives and lax.ppermute only.
A program may use at most 64 MiB of HBM per device.

```python
import math
import jax
import jax.numpy as jnp
from jax import lax

NORB = 128
NPROJ = 4
CX = 8
NY = 8
NZ = 128
ATOM_DEV = 8
SLOTS = 16
POINTS = 256
NX = 512
ATOMS = 512
SLOT_ROWS = 1024
CELLS = 524288
N_DOM = 64


def draw_slot_atom(key, part):
    domains = SLOT_ROWS // SLOTS
    domain_keys = jax.random.split(jax.random.fold_in(key, 11), domains)
    chosen = jax.vmap(lambda subkey: jax.random.permutation(subkey, 3 * ATOM_DEV)[:SLOTS])(domain_keys)
    vacant = jax.random.randint(jax.random.fold_in(key, 12), (domains, SLOTS), 0, 4) == 0
    return jnp.where(vacant, -1, chosen).reshape(-1).astype(jnp.int32)


def with_ends(result, own_key, low, largest):
    index_at = [jax.random.randint(jax.random.fold_in(own_key, axis), (), 0, length) for axis, length in enumerate(result.shape)]
    widest = result.shape.index(max(result.shape))
    next_to = index_at[:widest] + [(index_at[widest] + 1) % result.shape[widest]] + index_at[widest + 1:]
    return result.at[tuple(index_at)].set(low).at[tuple(next_to)].set(largest)


def steps_of(own_key, shape, pieces, least, top_value):
    loudness, own = 1.0, jax.random.fold_in(own_key, 6)
    for position, blocks in pieces:
        steps = jnp.exp(jax.random.uniform(jax.random.fold_in(own, position), (blocks,), jnp.float32, least / len(pieces), top_value / len(pieces)))
        loudness = loudness * jnp.repeat(steps, shape[position] // blocks).reshape([-1 if axis == position else 1 for axis in range(len(shape))])
    return loudness


def normal_values(own_key, shape, width, reach, shards=(), kind=jnp.bfloat16):
    values = width * jax.random.normal(own_key, shape, jnp.float32)
    if shards:
        values = values * steps_of(own_key, shape, shards, -0.22, 0.18)
    return jnp.clip(values, -reach, reach).astype(kind)


def setup_inputs(seed: int = 0) -> dict:
    key_list = jax.random.split(jax.random.key(seed), 7)
    return {
        "orbitals": normal_values(key_list[0], (NORB, NX, NY, NZ), 1.0, 6.0, ((0, 4), (1, 64)), jnp.float32),
        "potential": jnp.clip(jax.random.uniform(key_list[1], (NX, NY, NZ), jnp.float32, -1.0, 1.0) * steps_of(key_list[1], (NX, NY, NZ), ((0, 64),), -0.4, 0.0), -1.0, 1.0),
        "slot_atom": draw_slot_atom(jax.random.fold_in(key_list[6], 71), 0),
        "point_offset": with_ends(jax.random.randint(key_list[3], (SLOT_ROWS, POINTS), 0, CX * NY * NZ), jax.random.fold_in(key_list[3], 1), 0, (CX * NY * NZ) - 1).astype(jnp.int32),
        "projector": normal_values(key_list[4], (SLOT_ROWS, NPROJ, POINTS), (0.8 * POINTS ** -0.5), 0.3125, ((0, 64),), jnp.float32),
        "coupling": jnp.clip(jnp.exp(jax.random.uniform(key_list[5], (NPROJ,), jnp.float32, math.log(0.5), math.log(2.0))), 0.5, 2.0),
    }


stencil = (-5369.0 / 1800.0, 12.0 / 7.0, -15.0 / 56.0, 10.0 / 189.0, -1.0 / 112.0, 2.0 / 1925.0, -1.0 / 16632.0)
center = 9.0
half_width = 7.0
exact = lax.Precision.HIGHEST


def laplace(wavefield):
    summed = 3.0 * stencil[0] * wavefield
    for direction in (1, 2, 3):
        for distance in range(1, 7):
            summed = summed + stencil[distance] * (jnp.roll(wavefield, distance, direction) + jnp.roll(wavefield, -distance, direction))
    return summed


def nonlocal_term(flat_field, slot_atom, point_offset, projector, coupling):
    cells_dev = CX * NY * NZ
    domain_of = jnp.arange(SLOT_ROWS, dtype=jnp.int32) // SLOTS
    global_offset = (point_offset + (domain_of * cells_dev)[:, None]).astype(jnp.int32)
    sampled = flat_field[:, global_offset]
    partial_sums = jnp.einsum('gsp,sjp->sjg', sampled, projector, precision=exact)
    owner_domain = (domain_of + slot_atom // ATOM_DEV - 1) % N_DOM
    atom_index = jnp.where(slot_atom >= 0, owner_domain * ATOM_DEV + slot_atom % ATOM_DEV, ATOMS).astype(jnp.int32)
    totals = jax.ops.segment_sum(partial_sums, atom_index, num_segments=ATOMS + 1)
    live_atom = (jnp.arange(ATOMS + 1) < ATOMS)[:, None, None]
    coefficients = jnp.where(live_atom, totals * coupling[None, :, None], jnp.float32(0.0))
    per_slot = coefficients[atom_index]
    contribution = jnp.einsum('sjp,sjg->gsp', projector, per_slot, precision=exact)
    group_size = flat_field.shape[0]
    return jnp.zeros_like(flat_field).at[:, global_offset.reshape(-1)].add(contribution.reshape(group_size, -1))


def hamiltonian(wavefield, potential, slot_atom, point_offset, projector, coupling):
    group_size = wavefield.shape[0]
    nonlocal_part = nonlocal_term(wavefield.reshape(group_size, -1), slot_atom, point_offset, projector, coupling)
    return -0.5 * laplace(wavefield) + potential[None] * wavefield + nonlocal_part.reshape(wavefield.shape)


def reference(orbitals, potential, slot_atom, point_offset, projector, coupling):
    def apply_h(wavefield):
        return hamiltonian(wavefield, potential, slot_atom, point_offset, projector, coupling)

    def filter_group(wavefield):
        previous = wavefield
        current = (apply_h(wavefield) - center * wavefield) / half_width
        for degree in range(2, 5):
            following = 2.0 * (apply_h(current) - center * current) / half_width - previous
            previous, current = current, following
        return current, apply_h(current)

    grouped = orbitals.reshape(NORB // 8, 8, NX, NY, NZ)
    filtered_groups, image_groups = lax.map(filter_group, grouped)
    filtered = filtered_groups.reshape(NORB, NX, NY, NZ)
    flat_filtered = filtered.reshape(NORB, -1)
    flat_image = image_groups.reshape(NORB, -1)
    inverse_cells = 1.0 / CELLS
    margin = jnp.dot(flat_filtered, flat_filtered.T, preferred_element_type=jnp.float32, precision=exact) * inverse_cells
    projected = jnp.dot(flat_filtered, flat_image.T, preferred_element_type=jnp.float32, precision=exact) * inverse_cells
    return filtered, projected, margin
```

```python
import functools
import math

import jax
import jax.numpy as jnp
import numpy as np
from jax import lax
from jax.experimental import pallas as pl
from jax.experimental.pallas import tpu as pltpu
from jax.sharding import Mesh
from jax.sharding import PartitionSpec as P

STENCIL = (
    -5369.0 / 1800.0,
    12.0 / 7.0,
    -15.0 / 56.0,
    10.0 / 189.0,
    -1.0 / 112.0,
    2.0 / 1925.0,
    -1.0 / 16632.0,
)
CENTER = 9.0
HALF_WIDTH = 7.0
REACH = 6

LAYERS = 16
NY = 8
ORBS = 16
NZ = 128
ROWS = LAYERS * NY
EDGE = REACH * NY
F32 = jnp.float32
BF16 = jnp.bfloat16
NT = (((1,), (1,)), ((), ()))
NN = (((1,), (0,)), ((), ()))
Y_RING = ("yl", "yh")


def dot(a, b, dims=NN):
    return lax.dot_general(a, b, dims, preferred_element_type=F32)


def exact_dot(a, b, dims=NN):
    return lax.dot_general(
        a, b, dims, precision=lax.Precision.HIGHEST, preferred_element_type=F32
    )


def split(v):
    high = v.astype(BF16)
    return high, (v - high.astype(F32)).astype(BF16)


def vmem_call(kernel, out_shape, inputs, scalars=(), scratch=(), flops=0):
    many = isinstance(out_shape, (list, tuple))
    held = [*inputs, *(out_shape if many else [out_shape]), *scratch]
    limit = (4 << 20) + sum(math.prod(v.shape) * v.dtype.itemsize for v in held)
    specs = [pl.BlockSpec(memory_space=pltpu.SMEM)] * len(scalars)
    specs += [pl.BlockSpec(memory_space=pltpu.VMEM)] * len(inputs)
    out = pl.BlockSpec(memory_space=pltpu.VMEM)
    return pl.pallas_call(
        kernel,
        out_shape=out_shape,
        in_specs=specs,
        out_specs=[out] * len(out_shape) if many else out,
        scratch_shapes=list(scratch),
        compiler_params=pltpu.CompilerParams(vmem_limit_bytes=limit),
        cost_estimate=pl.CostEstimate(flops=flops, bytes_accessed=4 << 20, transcendentals=0),
    )(*scalars, *inputs)


def shape(*dims, dtype=F32):
    return jax.ShapeDtypeStruct(dims, dtype)


def projector_kernel(place_ref, own_ref, other_ref, dense_ref, table_ref, potential_ref, scratch):
    place = place_ref[0]
    row_of = lax.broadcasted_iota(jnp.int32, (64, 256), 0)
    lane_of = lax.broadcasted_iota(jnp.int32, (128, 256), 0)
    lane = lax.broadcasted_iota(jnp.int32, (4, 128), 1)
    which = lax.broadcasted_iota(jnp.int32, (4, 128), 0)
    for slab in range(2):
        own = place == slab
        owners = []
        for slot in range(16):
            atom = jnp.where(own, own_ref[slot, 5:6, :128], other_ref[slot, 5:6, :128]).astype(jnp.int32)
            match = (lane == (8 * slab + atom) * 4 + which) & (atom >= 0)
            owners.append(jnp.where(match, 1.0, 0.0))
        table_ref[slab] = jnp.concatenate(owners + owners, axis=0)

        def one_slot(slot, carry, slab=slab, own=own):
            static = jnp.where(own, own_ref[slot], other_ref[slot])
            for k in range(4):
                piece = static[6 + k // 2 : 7 + k // 2, (k % 2) * 128 : (k % 2) * 128 + 128]
                potential_ref[slab * 64 + slot * 4 + k] = piece
            cell = static[4:5].astype(jnp.int32)
            at_row = jnp.where(row_of == (cell >> 7), 1.0, 0.0).astype(BF16)
            at_lane = jnp.where(lane_of == (cell & 127), 1.0, 0.0).astype(BF16)
            high, low = split(static[:4])
            found = []
            for part in (high, low):
                spread = jnp.concatenate([at_row * part[j : j + 1, :] for j in range(4)], axis=0)
                found.append(dot(spread, at_lane, NT))
            found = found[0] + found[1]
            for j in range(4):
                scratch[pl.ds(slot * 4 + j, 64, stride=64), :] = found[j * 64 : (j + 1) * 64]
            return carry

        lax.fori_loop(0, 16, one_slot, 0, unroll=4)

        def one_row(xy, carry, slab=slab):
            high, low = split(scratch[pl.ds(pl.multiple_of(xy * 64, 64), 64), :])
            dense_ref[slab * 64 + xy] = jnp.concatenate([high, low], axis=0)
            return carry

        lax.fori_loop(0, 64, one_row, 0, unroll=8)


def rows_of(refs, start, count):
    pieces = []
    for ref, low, high in zip(refs, (0, EDGE, ROWS - EDGE), (EDGE, ROWS - EDGE, ROWS)):
        first, end = max(start, low), min(start + count, high)
        if first < end:
            pieces.append(ref[first - low : end - low])
    return pieces[0] if len(pieces) == 1 else jnp.concatenate(pieces, axis=0)


def begin_kernel(
    place_ref, atom_ref, orbitals_ref, potential_ref, cell_ref, proj_ref, own_ref, outgoing_ref, static_ref
):
    for slot in range(16):
        rows = potential_ref[slot * 4 : slot * 4 + 4]
        static_ref[slot] = jnp.concatenate(
            [
                proj_ref[slot],
                cell_ref[slot : slot + 1].astype(F32),
                jnp.full((1, 256), atom_ref[slot], jnp.int32).astype(F32),
                jnp.concatenate([rows[0:1], rows[1:2]], axis=1),
                jnp.concatenate([rows[2:3], rows[3:4]], axis=1),
            ],
            axis=0,
        )
    keep = place_ref[0] * (ORBS * 64)
    for xy in range(64):
        own_ref[xy] = orbitals_ref[pl.ds(keep + xy, ORBS, stride=64), :]
        outgoing_ref[xy] = orbitals_ref[pl.ds(ORBS * 64 - keep + xy, ORBS, stride=64), :]


def join_kernel(place_ref, odd_ref, own_ref, other_ref, left_ref, middle_ref, right_ref, *sends):
    for place in range(2):

        @pl.when(place_ref[0] == place)
        def _(place=place):
            first, second = (own_ref, other_ref) if place == 0 else (other_ref, own_ref)
            left_ref[...] = first[:EDGE]
            middle_ref[: 64 - EDGE] = first[EDGE:]
            middle_ref[64 - EDGE :] = second[: 64 - EDGE]
            right_ref[...] = second[64 - EDGE :]

    copy_faces(odd_ref, left_ref, right_ref, *sends)


def copy_faces(odd_ref, left_ref, right_ref, outer_ref, inner_ref):
    @pl.when(odd_ref[0] == 0)
    def _():
        outer_ref[...] = left_ref[...]
        inner_ref[...] = right_ref[...]

    @pl.when(odd_ref[0] == 1)
    def _():
        outer_ref[...] = right_ref[...]
        inner_ref[...] = left_ref[...]


def project_kernel(left_ref, middle_ref, right_ref, dense_ref, table_ref, *outs):
    refs = (left_ref, middle_ref, right_ref)
    owner = jnp.zeros((ORBS, 128), F32)
    for slab in range(2):
        total = jnp.zeros((32, 128), F32)
        for xy in range(slab * 64, slab * 64 + 64, 2):
            pair = rows_of(refs, xy, 2)
            high, low = split(jnp.concatenate([pair[0], pair[1]], axis=1))
            dense = jnp.concatenate([dense_ref[xy], dense_ref[xy + 1]], axis=1)
            total = total + dot(jnp.concatenate([high, low], axis=0), dense, NT)
        owner = owner + exact_dot(total[:ORBS] + total[ORBS:], table_ref[slab])
    for out in outs:
        out[...] = owner


def local_kernel(alpha, center, with_previous, *refs):
    field, (potential_ref, matrix_ref) = refs[:3], refs[3:5]
    previous, out_ref = refs[5:8], refs[-1]
    scale = -0.5 * alpha
    along_y = (
        STENCIL[1] * scale,
        (STENCIL[2] + STENCIL[6]) * scale,
        (STENCIL[3] + STENCIL[5]) * scale,
        2.0 * STENCIL[4] * scale,
    )
    diagonal = alpha * (-1.5 * STENCIL[0] - center)
    for x in range(LAYERS):
        v = rows_of(field, x * NY, NY)
        flat = v.reshape(NY * ORBS, NZ)
        high, low = split(flat)
        product = dot(jnp.concatenate([high, low], axis=1), matrix_ref[...])
        total = (product[:, :NZ] + product[:, NZ:]).reshape(NY, ORBS, NZ)
        weight = potential_ref[x * NY : (x + 1) * NY] * alpha + diagonal
        total = total + weight * v
        for distance in range(1, 4):
            up = jnp.concatenate([v[distance:], v[:distance]], axis=0)
            down = jnp.concatenate([v[NY - distance :], v[: NY - distance]], axis=0)
            total = total + along_y[distance - 1] * (up + down)
        total = total + along_y[3] * jnp.concatenate([v[4:], v[:4]], axis=0)
        for distance in range(1, REACH + 1):
            near = None
            for at in (x - distance, x + distance):
                if 0 <= at < LAYERS:
                    piece = rows_of(field, at * NY, NY)
                    near = piece if near is None else near + piece
            if near is not None:
                total = total + (STENCIL[distance] * scale) * near
        if with_previous:
            total = total - rows_of(previous, x * NY, NY)
        out_ref[x * NY : (x + 1) * NY] = total


def spread_kernel(
    alpha, odd_ref, local_ref, own_ref, outer_ref, inner_ref, dense_ref, table_ref, coupling_ref, *outs
):
    lane = lax.broadcasted_iota(jnp.int32, (ORBS, 128), 1)
    left_lanes = jnp.where(odd_ref[0] == 0, 0, 64)
    outer = pltpu.roll(outer_ref[...], 64, 1)
    inner = pltpu.roll(inner_ref[...], 64, 1)
    total = own_ref[...] + jnp.where((lane & 64) == left_lanes, outer, inner)
    coefficient = total * (coupling_ref[...] * alpha)

    def write(row, value):
        for ref, low, high in zip(outs, (0, EDGE, ROWS - EDGE), (EDGE, ROWS - EDGE, ROWS)):
            if low <= row < high:
                ref[row - low] = value

    for slab in range(2):
        per_slot = exact_dot(coefficient, table_ref[slab], NT)
        weights = jnp.concatenate(split(per_slot), axis=0)
        for xy in range(slab * 64, slab * 64 + 64, 2):
            dense = jnp.concatenate([dense_ref[xy], dense_ref[xy + 1]], axis=1)
            term = dot(weights, dense)
            term = term[:ORBS] + term[ORBS:]
            write(xy, local_ref[xy] + term[:, :NZ])
            write(xy + 1, local_ref[xy + 1] + term[:, NZ:])


def faces(alpha, odd_ref, left_ref, right_ref, outer_ref, inner_ref, write_left, write_right):
    scale = -0.5 * alpha
    for odd in range(2):

        @pl.when(odd_ref[0] == odd)
        def _(odd=odd):
            from_left, from_right = (inner_ref, outer_ref) if odd else (outer_ref, inner_ref)
            for x in range(REACH):
                value = left_ref[x * NY : (x + 1) * NY]
                for distance in range(x + 1, REACH + 1):
                    at = (x - distance + REACH) * NY
                    value = value + (STENCIL[distance] * scale) * from_left[at : at + NY]
                write_left(odd, x, value)
                value = right_ref[x * NY : (x + 1) * NY]
                for distance in range(REACH - x, REACH + 1):
                    at = (x + distance - REACH) * NY
                    value = value + (STENCIL[distance] * scale) * from_right[at : at + NY]
                write_right(odd, x, value)


def faces_kernel(alpha, odd_ref, left_ref, right_ref, outer_ref, inner_ref, *outs):
    left_out, right_out, outer_out, inner_out = outs

    def write_left(odd, x, value):
        for ref in (left_out, inner_out if odd else outer_out):
            ref[x * NY : (x + 1) * NY] = value

    def write_right(odd, x, value):
        for ref in (right_out, outer_out if odd else inner_out):
            ref[x * NY : (x + 1) * NY] = value

    faces(alpha, odd_ref, left_ref, right_ref, outer_ref, inner_ref, write_left, write_right)


def whole_faces_kernel(
    alpha, with_sends, odd_ref, place_ref, member_ref, left_ref, middle_ref, right_ref, outer_ref, inner_ref, *rest
):
    blocks, rest = rest[:4], rest[4:]
    if with_sends:
        whole_ref, return_ref, left_out, right_out, outer_out, inner_out = rest
    else:
        (whole_ref,) = rest

    def write_left(odd, x, value):
        whole_ref[x * NY : (x + 1) * NY] = value
        if with_sends:
            for ref in (left_out, inner_out if odd else outer_out):
                ref[x * NY : (x + 1) * NY] = value

    def write_right(odd, x, value):
        at = ROWS - EDGE + x * NY
        whole_ref[at : at + NY] = value
        if with_sends:
            for ref in (right_out, outer_out if odd else inner_out):
                ref[x * NY : (x + 1) * NY] = value

    faces(alpha, odd_ref, left_ref, right_ref, outer_ref, inner_ref, write_left, write_right)
    whole_ref[EDGE : ROWS - EDGE] = middle_ref[...]
    for step in range(4):
        blocks[step][...] = whole_ref[pl.ds(jnp.bitwise_xor(member_ref[0], step) * 32, 32)]
    if with_sends:
        return_ref[...] = whole_ref[pl.ds((1 - place_ref[0]) * 64, 64)]


def gram(left, both_ref):
    total = jnp.zeros((128, 256), F32)
    for xy in range(0, 32, 2):
        piece = [jnp.concatenate([ref[xy], ref[xy + 1]], axis=1) for ref in left]
        rows = jnp.concatenate(split(jnp.concatenate(piece, axis=0)), axis=0)
        columns = jnp.concatenate([both_ref[xy], both_ref[xy + 1]], axis=1)
        total = total + dot(rows, columns, NT)
    total = total[:64] + total[64:]
    return total[:, :128] + total[:, 128:]


def field_gram_kernel(member_ref, core_ref, *refs):
    own, others, both_ref, margin_ref = refs[:4], refs[4:8], refs[8], refs[9]
    for step in range(4):
        member = jnp.bitwise_xor(member_ref[0], step)
        for ref, core in ((own[step], core_ref[0]), (others[step], 1 - core_ref[0])):
            band = jnp.bitwise_and(member, 1) * 2 + core
            at = pl.multiple_of(band * (2 * ORBS) + (member >> 1) * ORBS, ORBS)
            for xy in range(32):
                high, low = split(ref[xy])
                both_ref[xy, pl.ds(at, ORBS), :] = high
                both_ref[xy, pl.ds(128 + at, ORBS), :] = low
    margin_ref[...] = gram(own, both_ref)


def image_gram_kernel(member_ref, *refs):
    images, both_ref, margin_ref, out_ref = refs[:4], refs[4], refs[5], refs[6]
    total = gram(images, both_ref)
    for step in range(4):
        member = jnp.bitwise_xor(member_ref[0], step)
        out_ref[member, :ORBS] = margin_ref[step * ORBS : (step + 1) * ORBS]
        out_ref[member, ORBS:] = total[step * ORBS : (step + 1) * ORBS]


def copies_kernel(in_ref, out_ref):
    total = (in_ref[0] + in_ref[1]) + (in_ref[2] + in_ref[3])
    for copy in range(out_ref.shape[0]):
        out_ref[copy] = total


def sum_kernel(copies_ref, out_ref):
    parts = [copies_ref[copy] for copy in range(copies_ref.shape[0])]
    while len(parts) > 1:
        parts = [a + b for a, b in zip(parts[::2], parts[1::2])]
    out_ref[...] = parts[0]


def restore_kernel(place_ref, own_ref, other_ref, out_ref):
    place = place_ref[0]
    for orb in range(ORBS):
        for layer in range(8):
            at = layer * 8 * ORBS + orb
            mine = own_ref[pl.ds(place * (64 * ORBS) + at, 8, stride=ORBS), :]
            out_ref[place * ORBS + orb, layer] = mine
            out_ref[(1 - place) * ORBS + orb, layer] = other_ref[pl.ds(at, 8, stride=ORBS), :]


def along_z(alpha):
    circulant = np.zeros((NZ, NZ), np.float64)
    for row in range(NZ):
        for distance in range(1, REACH + 1):
            circulant[row, (row + distance) % NZ] += STENCIL[distance]
            circulant[row, (row - distance) % NZ] += STENCIL[distance]
    circulant = (circulant * (-0.5 * alpha)).astype(np.float32)
    high = circulant.astype(jnp.bfloat16)
    low = (circulant - high.astype(np.float32)).astype(jnp.bfloat16)
    return jnp.asarray(np.block([[high, low], [high, low]]))


def swap(value, axis, count, bit):
    return lax.ppermute(value, axis, [(i, i ^ bit) for i in range(count)])


def trade(blocks):
    return [swap(block, Y_RING, 4, step) if step else block for step, block in enumerate(blocks)]


def meet(outer, inner, count):
    outer_pairs = [(i, (i + 1 if i % 2 else i - 1) % count) for i in range(count)]
    inner_pairs = [(i, i ^ 1) for i in range(count)]
    outer = lax.ppermute(outer, ("z", "x"), outer_pairs)
    return outer, lax.ppermute(inner, ("z", "x"), inner_pairs)


def in_order(place, own, other):
    return jnp.where(place == 0, jnp.stack([own, other]), jnp.stack([other, own]))


def shards(sizes, orbitals, potential, slot_atom, point_offset, projector, coupling):
    supers = sizes["z"] * sizes["x"]
    place = lax.axis_index("yl")
    place_1 = place.reshape(1).astype(jnp.int32)
    member_1 = lax.axis_index(Y_RING).reshape(1).astype(jnp.int32)
    core_1 = lax.axis_index("core").reshape(1).astype(jnp.int32)
    odd_1 = (lax.axis_index("x") % 2).reshape(1).astype(jnp.int32)
    coupling_row = jnp.tile(coupling, 32).reshape(1, 128)
    orbitals, place_1, member_1, core_1, odd_1, coupling_row = lax.optimization_barrier(
        (orbitals, place_1, member_1, core_1, odd_1, coupling_row)
    )

    block, half, field = (shape(rows, ORBS, NZ) for rows in (32, 64, ROWS))
    own, outgoing, static = vmem_call(
        begin_kernel,
        [half, half, shape(16, 8, 256)],
        (orbitals.reshape(2 * ORBS * 64, NZ), potential.reshape(64, NZ), point_offset, projector),
        scalars=(place_1, slot_atom),
        flops=1 << 20,
    )
    other_static = swap(static, "yl", 2, 1)
    other_orbitals = swap(outgoing, "yl", 2, 1)
    dense, table, potential_rows = vmem_call(
        projector_kernel,
        [shape(ROWS, 128, NZ, dtype=BF16), shape(2, 128, 128), shape(ROWS, 1, NZ)],
        (static, other_static),
        scalars=(place_1,),
        scratch=(pltpu.VMEM((64 * 64, NZ), F32),),
        flops=1 << 30,
    )
    face, middle = shape(EDGE, ORBS, NZ), shape(ROWS - 2 * EDGE, ORBS, NZ)
    three = [face, middle, face]
    dense, other_orbitals = lax.optimization_barrier((dense, other_orbitals))
    *current, outer, inner = vmem_call(
        join_kernel, three + [face, face], (own, other_orbitals), scalars=(place_1, odd_1), flops=1 << 20
    )
    previous = None
    for degree in range(5):
        last = degree == 4
        alpha = 1.0 if last else (2.0 if degree else 1.0) / HALF_WIDTH
        center = 0.0 if last else CENTER
        with_previous = degree > 0 and not last
        outer, inner = meet(outer, inner, supers)
        if last:
            fields = trade(blocks)
        outer_sums, inner_sums = vmem_call(
            project_kernel, [shape(ORBS, 128)] * 2, (*current, dense, table), flops=1 << 29
        )
        sums = outer_sums
        outer_sums, inner_sums = meet(outer_sums, inner_sums, supers)
        local = vmem_call(
            functools.partial(local_kernel, alpha, center, with_previous),
            field,
            (*current, potential_rows, along_z(alpha)) + (tuple(previous) if with_previous else ()),
            flops=1 << 30,
        )
        left, center_rows, right = vmem_call(
            functools.partial(spread_kernel, alpha),
            three,
            (local, sums, outer_sums, inner_sums, dense, table, coupling_row),
            scalars=(odd_1,),
            flops=1 << 29,
        )
        if degree < 3:
            left, right, outer, inner = vmem_call(
                functools.partial(faces_kernel, alpha),
                [face] * 4,
                (left, right, outer, inner),
                scalars=(odd_1,),
                flops=1 << 24,
            )
            previous, current = current, [left, center_rows, right]
        elif degree == 3:
            *blocks, filtered, returning, left, right, outer, inner = vmem_call(
                functools.partial(whole_faces_kernel, alpha, True),
                [block] * 4 + [field, half] + [face] * 4,
                (left, center_rows, right, outer, inner),
                scalars=(odd_1, place_1, member_1),
                flops=1 << 24,
            )
            previous, current = current, [left, center_rows, right]
        else:
            left, center_rows, right, outer, inner, *fields = lax.optimization_barrier(
                (left, center_rows, right, outer, inner, *fields)
            )
            blocks = vmem_call(
                functools.partial(whole_faces_kernel, alpha, False),
                [block] * 4,
                (left, center_rows, right, outer, inner),
                scalars=(odd_1, place_1, member_1),
                scratch=(pltpu.VMEM((ROWS, ORBS, NZ), F32),),
                flops=1 << 24,
            )

    images = trade(blocks)
    others = [swap(value, "core", 2, 1) for value in fields]
    both, margins = vmem_call(
        field_gram_kernel,
        [shape(32, 256, NZ, dtype=BF16), shape(4 * ORBS, 128)],
        (*fields, *others),
        scalars=(member_1, core_1),
        flops=1 << 29,
    )
    products = vmem_call(
        image_gram_kernel,
        shape(4, 2 * ORBS, 128),
        (*images, both, margins),
        scalars=(member_1,),
        flops=1 << 29,
    )

    returning, products = lax.optimization_barrier((returning, products))
    returned = swap(returning, "yl", 2, 1)
    restored = vmem_call(
        restore_kernel,
        shape(2 * ORBS, 8, NY, NZ),
        (filtered.reshape(ROWS * ORBS, NZ), returned.reshape(64 * ORBS, NZ)),
        scalars=(place_1,),
        flops=1 << 20,
    )

    products = lax.all_to_all(products, Y_RING, 0, 0, tiled=True)
    copies = vmem_call(copies_kernel, shape(supers, 2 * ORBS, 128), (products,), flops=1 << 20)
    copies = lax.all_to_all(copies, ("z", "x"), 0, 0, tiled=True)
    total = vmem_call(sum_kernel, shape(2 * ORBS, 128), (copies,), flops=1 << 20)
    total = total.reshape(2, ORBS, 128)
    total, restored = lax.optimization_barrier((total, restored))
    total = in_order(place, total, swap(total, "yl", 2, 1))
    inverse_cells = 1.0 / (supers * LAYERS * NY * NZ)
    margin = (total[:, 0] * inverse_cells).reshape(2 * ORBS, 128).T
    projected = (total[:, 1] * inverse_cells).reshape(2 * ORBS, 128).T
    return restored, projected, margin


def solution(mesh):
    sizes = {"z": 8, "x": 4, "yl": 2, "yh": 2, "core": 2}
    fine = Mesh(mesh.devices.reshape(tuple(sizes.values())), tuple(sizes))
    dom, band = ("z", "x", "yl"), ("yh", "core")
    in_specs = (
        P(band, dom, None, None),
        P(dom, None, None),
        P(dom),
        P(dom, None),
        P(dom, None, None),
        P(),
    )
    out_specs = (P(band, dom, None, None), P(None, band), P(None, band))
    return jax.shard_map(
        functools.partial(shards, sizes),
        mesh=fine,
        in_specs=in_specs,
        out_specs=out_specs,
        check_vma=False,
    )
```

```python
import functools
import math

import jax
import jax.numpy as jnp
import numpy as np
from jax import lax
from jax.experimental import pallas as pl
from jax.experimental.pallas import tpu as pltpu
from jax.sharding import Mesh
from jax.sharding import PartitionSpec as P

STENCIL = (
    -5369.0 / 1800.0,
    12.0 / 7.0,
    -15.0 / 56.0,
    10.0 / 189.0,
    -1.0 / 112.0,
    2.0 / 1925.0,
    -1.0 / 16632.0,
)
CENTER = 9.0
HALF_WIDTH = 7.0
REACH = 6

LAYERS = 16
NY = 8
ORBS = 16
NZ = 128
ROWS = LAYERS * NY
EDGE = REACH * NY
F32 = jnp.float32
BF16 = jnp.bfloat16
NT = (((1,), (1,)), ((), ()))
NN = (((1,), (0,)), ((), ()))
Y_RING = ("yl", "yh")
STEPS = (0, 2, 3, 1)


def dot(a, b, dims=NN):
    return lax.dot_general(a, b, dims, preferred_element_type=F32)


def exact_dot(a, b, dims=NN):
    return lax.dot_general(
        a, b, dims, precision=lax.Precision.HIGHEST, preferred_element_type=F32
    )


def split(v):
    high = v.astype(BF16)
    return high, (v - high.astype(F32)).astype(BF16)


def vmem_call(kernel, out_shape, inputs, scalars=(), scratch=(), flops=0, space=pltpu.VMEM):
    many = isinstance(out_shape, (list, tuple))
    held = [*inputs, *(out_shape if many else [out_shape])]
    limit = (6 << 20) + sum(math.prod(v.shape) * v.dtype.itemsize for v in held)
    if space == pltpu.HBM:
        limit = 60 << 20
    specs = [pl.BlockSpec(memory_space=pltpu.SMEM)] * len(scalars)
    specs += [pl.BlockSpec(memory_space=space)] * len(inputs)
    out = pl.BlockSpec(memory_space=pltpu.VMEM)
    return pl.pallas_call(
        kernel,
        out_shape=out_shape,
        in_specs=specs,
        out_specs=[out] * len(out_shape) if many else out,
        scratch_shapes=list(scratch),
        compiler_params=pltpu.CompilerParams(vmem_limit_bytes=limit),
        cost_estimate=pl.CostEstimate(flops=flops, bytes_accessed=4 << 20, transcendentals=0),
    )(*scalars, *inputs)


def shape(*dims, dtype=F32):
    return jax.ShapeDtypeStruct(dims, dtype)


def projector_kernel(
    place_ref, coupling_ref, own_ref, other_ref, dense_ref, table_ref, potential_ref, row_ref, scratch
):
    place = place_ref[0]
    row_of = lax.broadcasted_iota(jnp.int32, (64, 256), 0)
    lane_of = lax.broadcasted_iota(jnp.int32, (128, 256), 0)
    lane = lax.broadcasted_iota(jnp.int32, (4, 128), 1)
    which = lax.broadcasted_iota(jnp.int32, (4, 128), 0)
    row = jnp.zeros((1, 128), F32)
    for j in range(4):
        row = jnp.where((lane[:1] & 3) == j, coupling_ref[j], row)
    row_ref[...] = row
    for slab in range(2):
        own = place == slab
        owners = []
        for slot in range(16):
            atom = jnp.where(own, own_ref[slot, 5:6, :128], other_ref[slot, 5:6, :128]).astype(jnp.int32)
            match = (lane == (8 * slab + atom) * 4 + which) & (atom >= 0)
            owners.append(jnp.where(match, 1.0, 0.0))
        table_ref[slab] = jnp.concatenate(owners + owners, axis=0)

        def one_slot(slot, carry, slab=slab, own=own):
            static = jnp.where(own, own_ref[slot], other_ref[slot])
            for k in range(4):
                piece = static[6 + k // 2 : 7 + k // 2, (k % 2) * 128 : (k % 2) * 128 + 128]
                potential_ref[slab * 64 + slot * 4 + k] = piece
            cell = static[4:5].astype(jnp.int32)
            at_row = jnp.where(row_of == (cell >> 7), 1.0, 0.0).astype(BF16)
            at_lane = jnp.where(lane_of == (cell & 127), 1.0, 0.0).astype(BF16)
            high, low = split(static[:4])
            found = []
            for part in (high, low):
                spread = jnp.concatenate([at_row * part[j : j + 1, :] for j in range(4)], axis=0)
                found.append(dot(spread, at_lane, NT))
            found = found[0] + found[1]
            for j in range(4):
                scratch[pl.ds(slot * 4 + j, 64, stride=64), :] = found[j * 64 : (j + 1) * 64]
            return carry

        lax.fori_loop(0, 16, one_slot, 0, unroll=4)

        def one_row(xy, carry, slab=slab):
            high, low = split(scratch[pl.ds(pl.multiple_of(xy * 64, 64), 64), :])
            dense_ref[slab * 64 + xy] = jnp.concatenate([high, low], axis=0)
            return carry

        lax.fori_loop(0, 64, one_row, 0, unroll=8)


def rows_of(refs, start, count):
    pieces = []
    for ref, low, high in zip(refs, (0, EDGE, ROWS - EDGE), (EDGE, ROWS - EDGE, ROWS)):
        first, end = max(start, low), min(start + count, high)
        if first < end:
            pieces.append(ref[first - low : end - low])
    return pieces[0] if len(pieces) == 1 else jnp.concatenate(pieces, axis=0)


def fetch(sources, targets, sems):
    copies = [
        pltpu.make_async_copy(source, target, sems.at[k])
        for k, (source, target) in enumerate(zip(sources, targets))
    ]
    for copy in copies:
        copy.start()
    for copy in copies:
        copy.wait()


def static_kernel(atom_hbm, potential_hbm, cell_hbm, proj_hbm, static_ref, *scratch):
    atom_ref, potential_ref, cell_ref, proj_ref, sems = scratch
    fetch((atom_hbm, potential_hbm, cell_hbm, proj_hbm), scratch[:4], sems)
    for slot in range(16):
        rows = potential_ref[slot * 4 : slot * 4 + 4]
        static_ref[slot] = jnp.concatenate(
            [
                proj_ref[slot],
                cell_ref[slot : slot + 1].astype(F32),
                jnp.full((1, 256), atom_ref[slot], jnp.int32).astype(F32),
                jnp.concatenate([rows[0:1], rows[1:2]], axis=1),
                jnp.concatenate([rows[2:3], rows[3:4]], axis=1),
            ],
            axis=0,
        )


def half_kernel(which_ref, orbitals_hbm, half_ref, orbitals_ref, sems):
    start = pl.multiple_of(which_ref[0] * (ORBS * 64), ORBS * 64)
    fetch((orbitals_hbm.at[pl.ds(start, ORBS * 64)],), (orbitals_ref,), sems)
    for xy in range(64):
        half_ref[xy] = orbitals_ref[pl.ds(xy, ORBS, stride=64), :]


def join_kernel(place_ref, odd_ref, own_ref, other_ref, left_ref, middle_ref, right_ref, *sends):
    for place in range(2):

        @pl.when(place_ref[0] == place)
        def _(place=place):
            first, second = (own_ref, other_ref) if place == 0 else (other_ref, own_ref)
            left_ref[...] = first[:EDGE]
            middle_ref[: 64 - EDGE] = first[EDGE:]
            middle_ref[64 - EDGE :] = second[: 64 - EDGE]
            right_ref[...] = second[64 - EDGE :]

    copy_faces(odd_ref, left_ref, right_ref, *sends)


def copy_faces(odd_ref, left_ref, right_ref, outer_ref, inner_ref):
    @pl.when(odd_ref[0] == 0)
    def _():
        outer_ref[...] = left_ref[...]
        inner_ref[...] = right_ref[...]

    @pl.when(odd_ref[0] == 1)
    def _():
        outer_ref[...] = right_ref[...]
        inner_ref[...] = left_ref[...]


def project_kernel(left_ref, middle_ref, right_ref, dense_ref, table_ref, *outs):
    refs = (left_ref, middle_ref, right_ref)
    owner = jnp.zeros((ORBS, 128), F32)
    for slab in range(2):
        total = jnp.zeros((32, 128), F32)
        for xy in range(slab * 64, slab * 64 + 64, 2):
            pair = rows_of(refs, xy, 2)
            high, low = split(jnp.concatenate([pair[0], pair[1]], axis=1))
            dense = jnp.concatenate([dense_ref[xy], dense_ref[xy + 1]], axis=1)
            total = total + dot(jnp.concatenate([high, low], axis=0), dense, NT)
        owner = owner + exact_dot(total[:ORBS] + total[ORBS:], table_ref[slab])
    for out in outs:
        out[...] = owner


def local_kernel(alpha, center, with_previous, *refs):
    field, (potential_ref, matrix_ref) = refs[:3], refs[3:5]
    previous, out_ref = refs[5:8], refs[-1]
    scale = -0.5 * alpha
    along_y = (
        STENCIL[1] * scale,
        (STENCIL[2] + STENCIL[6]) * scale,
        (STENCIL[3] + STENCIL[5]) * scale,
        2.0 * STENCIL[4] * scale,
    )
    diagonal = alpha * (-1.5 * STENCIL[0] - center)
    for x in range(LAYERS):
        v = rows_of(field, x * NY, NY)
        flat = v.reshape(NY * ORBS, NZ)
        high, low = split(flat)
        product = dot(jnp.concatenate([high, low], axis=1), matrix_ref[...])
        total = (product[:, :NZ] + product[:, NZ:]).reshape(NY, ORBS, NZ)
        weight = potential_ref[x * NY : (x + 1) * NY] * alpha + diagonal
        total = total + weight * v
        for distance in range(1, 4):
            up = jnp.concatenate([v[distance:], v[:distance]], axis=0)
            down = jnp.concatenate([v[NY - distance :], v[: NY - distance]], axis=0)
            total = total + along_y[distance - 1] * (up + down)
        total = total + along_y[3] * jnp.concatenate([v[4:], v[:4]], axis=0)
        for distance in range(1, REACH + 1):
            near = None
            for at in (x - distance, x + distance):
                if 0 <= at < LAYERS:
                    piece = rows_of(field, at * NY, NY)
                    near = piece if near is None else near + piece
            if near is not None:
                total = total + (STENCIL[distance] * scale) * near
        if with_previous:
            total = total - rows_of(previous, x * NY, NY)
        out_ref[x * NY : (x + 1) * NY] = total


def spread_kernel(
    alpha, odd_ref, local_ref, own_ref, outer_ref, inner_ref, dense_ref, table_ref, coupling_ref, *outs
):
    lane = lax.broadcasted_iota(jnp.int32, (ORBS, 128), 1)
    left_lanes = jnp.where(odd_ref[0] == 0, 0, 64)
    outer = pltpu.roll(outer_ref[...], 64, 1)
    inner = pltpu.roll(inner_ref[...], 64, 1)
    total = own_ref[...] + jnp.where((lane & 64) == left_lanes, outer, inner)
    coefficient = total * (coupling_ref[...] * alpha)

    def write(row, value):
        for ref, low, high in zip(outs, (0, EDGE, ROWS - EDGE), (EDGE, ROWS - EDGE, ROWS)):
            if low <= row < high:
                ref[row - low] = value

    for slab in range(2):
        per_slot = exact_dot(coefficient, table_ref[slab], NT)
        weights = jnp.concatenate(split(per_slot), axis=0)
        for xy in range(slab * 64, slab * 64 + 64, 2):
            dense = jnp.concatenate([dense_ref[xy], dense_ref[xy + 1]], axis=1)
            term = dot(weights, dense)
            term = term[:ORBS] + term[ORBS:]
            write(xy, local_ref[xy] + term[:, :NZ])
            write(xy + 1, local_ref[xy + 1] + term[:, NZ:])


def faces(alpha, odd_ref, left_ref, right_ref, outer_ref, inner_ref, write_left, write_right):
    scale = -0.5 * alpha
    for odd in range(2):

        @pl.when(odd_ref[0] == odd)
        def _(odd=odd):
            from_left, from_right = (inner_ref, outer_ref) if odd else (outer_ref, inner_ref)
            for x in range(REACH):
                value = left_ref[x * NY : (x + 1) * NY]
                for distance in range(x + 1, REACH + 1):
                    at = (x - distance + REACH) * NY
                    value = value + (STENCIL[distance] * scale) * from_left[at : at + NY]
                write_left(odd, x, value)
                value = right_ref[x * NY : (x + 1) * NY]
                for distance in range(REACH - x, REACH + 1):
                    at = (x + distance - REACH) * NY
                    value = value + (STENCIL[distance] * scale) * from_right[at : at + NY]
                write_right(odd, x, value)


def faces_kernel(alpha, odd_ref, left_ref, right_ref, outer_ref, inner_ref, *outs):
    left_out, right_out, outer_out, inner_out = outs

    def write_left(odd, x, value):
        for ref in (left_out, inner_out if odd else outer_out):
            ref[x * NY : (x + 1) * NY] = value

    def write_right(odd, x, value):
        for ref in (right_out, outer_out if odd else inner_out):
            ref[x * NY : (x + 1) * NY] = value

    faces(alpha, odd_ref, left_ref, right_ref, outer_ref, inner_ref, write_left, write_right)


def whole_faces_kernel(
    alpha, with_sends, odd_ref, place_ref, member_ref, left_ref, middle_ref, right_ref, outer_ref, inner_ref, *rest
):
    blocks, rest = rest[:4], rest[4:]
    if with_sends:
        whole_ref, return_ref, left_out, right_out, outer_out, inner_out = rest
    else:
        (whole_ref,) = rest

    def write_left(odd, x, value):
        whole_ref[x * NY : (x + 1) * NY] = value
        if with_sends:
            for ref in (left_out, inner_out if odd else outer_out):
                ref[x * NY : (x + 1) * NY] = value

    def write_right(odd, x, value):
        at = ROWS - EDGE + x * NY
        whole_ref[at : at + NY] = value
        if with_sends:
            for ref in (right_out, outer_out if odd else inner_out):
                ref[x * NY : (x + 1) * NY] = value

    faces(alpha, odd_ref, left_ref, right_ref, outer_ref, inner_ref, write_left, write_right)
    whole_ref[EDGE : ROWS - EDGE] = middle_ref[...]
    for step, ref in zip(STEPS, blocks):
        ref[...] = whole_ref[pl.ds(jnp.bitwise_xor(member_ref[0], step) * 32, 32)]
    if with_sends:
        return_ref[...] = whole_ref[pl.ds((1 - place_ref[0]) * 64, 64)]


def gram(left, both_ref):
    total = jnp.zeros((128, 256), F32)
    for xy in range(0, 32, 2):
        piece = [jnp.concatenate([ref[xy], ref[xy + 1]], axis=1) for ref in left]
        rows = jnp.concatenate(split(jnp.concatenate(piece, axis=0)), axis=0)
        columns = jnp.concatenate([both_ref[xy], both_ref[xy + 1]], axis=1)
        total = total + dot(rows, columns, NT)
    total = total[:64] + total[64:]
    return total[:, :128] + total[:, 128:]


def field_gram_kernel(member_ref, core_ref, *refs):
    own, others, both_ref, margin_ref = refs[:4], refs[4:8], refs[8], refs[9]
    for k, step in enumerate(STEPS):
        member = jnp.bitwise_xor(member_ref[0], step)
        for ref, core in ((own[k], core_ref[0]), (others[k], 1 - core_ref[0])):
            band = jnp.bitwise_and(member, 1) * 2 + core
            at = pl.multiple_of(band * (2 * ORBS) + (member >> 1) * ORBS, ORBS)
            for xy in range(32):
                high, low = split(ref[xy])
                both_ref[xy, pl.ds(at, ORBS), :] = high
                both_ref[xy, pl.ds(128 + at, ORBS), :] = low
    margin_ref[...] = gram(own, both_ref)


def image_gram_kernel(member_ref, *refs):
    images, both_ref, margin_ref, out_ref = refs[:4], refs[4], refs[5], refs[6]
    total = gram(images, both_ref)
    for k, step in enumerate(STEPS):
        member = jnp.bitwise_xor(member_ref[0], step)
        out_ref[member, :ORBS] = margin_ref[k * ORBS : (k + 1) * ORBS]
        out_ref[member, ORBS:] = total[k * ORBS : (k + 1) * ORBS]


def copies_kernel(in_ref, out_ref):
    total = (in_ref[0] + in_ref[1]) + (in_ref[2] + in_ref[3])
    for copy in range(out_ref.shape[0]):
        out_ref[copy] = total


def sum_kernel(copies_ref, out_ref):
    parts = [copies_ref[copy] for copy in range(copies_ref.shape[0])]
    while len(parts) > 1:
        parts = [a + b for a, b in zip(parts[::2], parts[1::2])]
    out_ref[...] = parts[0]


def restore_kernel(place_ref, own_ref, other_ref, out_ref):
    place = place_ref[0]
    for orb in range(ORBS):
        for layer in range(8):
            at = layer * 8 * ORBS + orb
            mine = own_ref[pl.ds(place * (64 * ORBS) + at, 8, stride=ORBS), :]
            out_ref[place * ORBS + orb, layer] = mine
            out_ref[(1 - place) * ORBS + orb, layer] = other_ref[pl.ds(at, 8, stride=ORBS), :]


def along_z(alpha):
    circulant = np.zeros((NZ, NZ), np.float64)
    for row in range(NZ):
        for distance in range(1, REACH + 1):
            circulant[row, (row + distance) % NZ] += STENCIL[distance]
            circulant[row, (row - distance) % NZ] += STENCIL[distance]
    circulant = (circulant * (-0.5 * alpha)).astype(np.float32)
    high = circulant.astype(jnp.bfloat16)
    low = (circulant - high.astype(np.float32)).astype(jnp.bfloat16)
    return jnp.asarray(np.block([[high, low], [high, low]]))


def swap(value, axis, count, bit):
    return lax.ppermute(value, axis, [(i, i ^ bit) for i in range(count)])


def trade(blocks):
    return [swap(block, Y_RING, 4, step) if step else block for step, block in zip(STEPS, blocks)]


def meet(outer, inner, count):
    outer_pairs = [(i, (i + 1 if i % 2 else i - 1) % count) for i in range(count)]
    inner_pairs = [(i, i ^ 1) for i in range(count)]
    outer = lax.ppermute(outer, ("z", "x"), outer_pairs)
    return outer, lax.ppermute(inner, ("z", "x"), inner_pairs)


def in_order(place, own, other):
    return jnp.where(place == 0, jnp.stack([own, other]), jnp.stack([other, own]))


def shards(sizes, orbitals, potential, slot_atom, point_offset, projector, coupling):
    supers = sizes["z"] * sizes["x"]
    place = lax.axis_index("yl")
    place_1 = place.reshape(1).astype(jnp.int32)
    member_1 = lax.axis_index(Y_RING).reshape(1).astype(jnp.int32)
    core_1 = lax.axis_index("core").reshape(1).astype(jnp.int32)
    odd_1 = (lax.axis_index("x") % 2).reshape(1).astype(jnp.int32)
    block, half, field = (shape(rows, ORBS, NZ) for rows in (32, 64, ROWS))
    static = vmem_call(
        static_kernel,
        shape(16, 8, 256),
        (slot_atom, potential.reshape(64, NZ), point_offset, projector),
        scratch=(
            pltpu.SMEM((16,), jnp.int32),
            pltpu.VMEM((64, NZ), F32),
            pltpu.VMEM((16, 256), jnp.int32),
            pltpu.VMEM((16, 4, 256), F32),
            pltpu.SemaphoreType.DMA((4,)),
        ),
        flops=1 << 20,
        space=pltpu.HBM,
    )
    static, place_1, member_1, core_1, odd_1 = lax.optimization_barrier(
        (static, place_1, member_1, core_1, odd_1)
    )
    other_static = swap(static, "yl", 2, 1)

    def take(which):
        return vmem_call(
            half_kernel,
            half,
            (orbitals.reshape(2 * ORBS * 64, NZ),),
            scalars=(which,),
            scratch=(pltpu.VMEM((ORBS * 64, NZ), F32), pltpu.SemaphoreType.DMA((1,))),
            flops=1 << 20,
            space=pltpu.HBM,
        )

    outgoing, other_static = lax.optimization_barrier((take(1 - place_1), other_static))
    other_orbitals = swap(outgoing, "yl", 2, 1)
    own = take(place_1)
    dense, table, potential_rows, coupling_row = vmem_call(
        projector_kernel,
        [shape(ROWS, 128, NZ, dtype=BF16), shape(2, 128, 128), shape(ROWS, 1, NZ), shape(1, 128)],
        (static, other_static),
        scalars=(place_1, coupling),
        scratch=(pltpu.VMEM((64 * 64, NZ), F32),),
        flops=1 << 30,
    )
    face, middle = shape(EDGE, ORBS, NZ), shape(ROWS - 2 * EDGE, ORBS, NZ)
    three = [face, middle, face]
    dense, other_orbitals = lax.optimization_barrier((dense, other_orbitals))
    *current, outer, inner = vmem_call(
        join_kernel, three + [face, face], (own, other_orbitals), scalars=(place_1, odd_1), flops=1 << 20
    )
    previous = None
    for degree in range(5):
        last = degree == 4
        alpha = 1.0 if last else (2.0 if degree else 1.0) / HALF_WIDTH
        center = 0.0 if last else CENTER
        with_previous = degree > 0 and not last
        outer, inner = meet(outer, inner, supers)
        if last:
            fields = trade(blocks)
        outer_sums, inner_sums = vmem_call(
            project_kernel, [shape(ORBS, 128)] * 2, (*current, dense, table), flops=1 << 29
        )
        sums = outer_sums
        outer_sums, inner_sums = meet(outer_sums, inner_sums, supers)
        local = vmem_call(
            functools.partial(local_kernel, alpha, center, with_previous),
            field,
            (*current, potential_rows, along_z(alpha)) + (tuple(previous) if with_previous else ()),
            flops=1 << 30,
        )
        left, center_rows, right = vmem_call(
            functools.partial(spread_kernel, alpha),
            three,
            (local, sums, outer_sums, inner_sums, dense, table, coupling_row),
            scalars=(odd_1,),
            flops=1 << 29,
        )
        if degree < 3:
            left, right, outer, inner = vmem_call(
                functools.partial(faces_kernel, alpha),
                [face] * 4,
                (left, right, outer, inner),
                scalars=(odd_1,),
                flops=1 << 24,
            )
            previous, current = current, [left, center_rows, right]
        elif degree == 3:
            *blocks, filtered, returning, left, right, outer, inner = vmem_call(
                functools.partial(whole_faces_kernel, alpha, True),
                [block] * 4 + [field, half] + [face] * 4,
                (left, center_rows, right, outer, inner),
                scalars=(odd_1, place_1, member_1),
                flops=1 << 24,
            )
            previous, current = current, [left, center_rows, right]
        else:
            left, center_rows, right, outer, inner, *fields = lax.optimization_barrier(
                (left, center_rows, right, outer, inner, *fields)
            )
            blocks = vmem_call(
                functools.partial(whole_faces_kernel, alpha, False),
                [block] * 4,
                (left, center_rows, right, outer, inner),
                scalars=(odd_1, place_1, member_1),
                scratch=(pltpu.VMEM((ROWS, ORBS, NZ), F32),),
                flops=1 << 24,
            )

    images = trade(blocks)
    others = [swap(value, "core", 2, 1) for value in fields]
    both, margins = vmem_call(
        field_gram_kernel,
        [shape(32, 256, NZ, dtype=BF16), shape(4 * ORBS, 128)],
        (*fields, *others),
        scalars=(member_1, core_1),
        flops=1 << 29,
    )
    products = vmem_call(
        image_gram_kernel,
        shape(4, 2 * ORBS, 128),
        (*images, both, margins),
        scalars=(member_1,),
        flops=1 << 29,
    )

    products = lax.all_to_all(products, Y_RING, 0, 0, tiled=True)

    returning, products = lax.optimization_barrier((returning, products))
    returned = swap(returning, "yl", 2, 1)
    restored = vmem_call(
        restore_kernel,
        shape(2 * ORBS, 8, NY, NZ),
        (filtered.reshape(ROWS * ORBS, NZ), returned.reshape(64 * ORBS, NZ)),
        scalars=(place_1,),
        flops=1 << 34,
    )

    copies = vmem_call(copies_kernel, shape(supers, 2 * ORBS, 128), (products,), flops=1 << 20)
    copies = lax.all_to_all(copies, ("z", "x"), 0, 0, tiled=True)
    total = vmem_call(sum_kernel, shape(2 * ORBS, 128), (copies,), flops=1 << 20)
    total = total.reshape(2, ORBS, 128)
    total, restored = lax.optimization_barrier((total, restored))
    total = in_order(place, total, swap(total, "yl", 2, 1))
    inverse_cells = 1.0 / (supers * LAYERS * NY * NZ)
    margin = (total[:, 0] * inverse_cells).reshape(2 * ORBS, 128).T
    projected = (total[:, 1] * inverse_cells).reshape(2 * ORBS, 128).T
    return restored, projected, margin


def solution(mesh):
    sizes = {"z": 8, "x": 4, "yl": 2, "yh": 2, "core": 2}
    fine = Mesh(mesh.devices.reshape(tuple(sizes.values())), tuple(sizes))
    dom, band = ("z", "x", "yl"), ("yh", "core")
    in_specs = (
        P(band, dom, None, None),
        P(dom, None, None),
        P(dom),
        P(dom, None),
        P(dom, None, None),
        P(),
    )
    out_specs = (P(band, dom, None, None), P(None, band), P(None, band))
    return jax.shard_map(
        functools.partial(shards, sizes),
        mesh=fine,
        in_specs=in_specs,
        out_specs=out_specs,
        check_vma=False,
    )
```

```python
import functools
import math

import jax
import jax.numpy as jnp
import numpy as np
from jax import lax
from jax.experimental import pallas as pl
from jax.experimental.pallas import tpu as pltpu
from jax.sharding import Mesh
from jax.sharding import PartitionSpec as P

STENCIL = (
    -5369.0 / 1800.0,
    12.0 / 7.0,
    -15.0 / 56.0,
    10.0 / 189.0,
    -1.0 / 112.0,
    2.0 / 1925.0,
    -1.0 / 16632.0,
)
CENTER = 9.0
HALF_WIDTH = 7.0
REACH = 6

LAYERS = 16
NY = 8
ORBS = 16
NZ = 128
ROWS = LAYERS * NY
EDGE = REACH * NY
F32 = jnp.float32
BF16 = jnp.bfloat16
NT = (((1,), (1,)), ((), ()))
NN = (((1,), (0,)), ((), ()))
Y_RING = ("yl", "yh")
STEPS = (0, 2, 3, 1)


def dot(a, b, dims=NN):
    return lax.dot_general(a, b, dims, preferred_element_type=F32)


def exact_dot(a, b, dims=NN):
    return lax.dot_general(
        a, b, dims, precision=lax.Precision.HIGHEST, preferred_element_type=F32
    )


def split(v):
    high = v.astype(BF16)
    return high, (v - high.astype(F32)).astype(BF16)


def vmem_call(kernel, out_shape, inputs, scalars=(), scratch=(), flops=0, space=pltpu.VMEM):
    many = isinstance(out_shape, (list, tuple))
    held = [*inputs, *(out_shape if many else [out_shape])]
    limit = (6 << 20) + sum(math.prod(v.shape) * v.dtype.itemsize for v in held)
    if space == pltpu.HBM:
        limit = 60 << 20
    specs = [pl.BlockSpec(memory_space=pltpu.SMEM)] * len(scalars)
    specs += [pl.BlockSpec(memory_space=space)] * len(inputs)
    out = pl.BlockSpec(memory_space=pltpu.VMEM)
    return pl.pallas_call(
        kernel,
        out_shape=out_shape,
        in_specs=specs,
        out_specs=[out] * len(out_shape) if many else out,
        scratch_shapes=list(scratch),
        compiler_params=pltpu.CompilerParams(vmem_limit_bytes=limit),
        cost_estimate=pl.CostEstimate(flops=flops, bytes_accessed=4 << 20, transcendentals=0),
    )(*scalars, *inputs)


def shape(*dims, dtype=F32):
    return jax.ShapeDtypeStruct(dims, dtype)


def projector_kernel(
    place_ref, coupling_ref, own_ref, other_ref, dense_ref, table_ref, potential_ref, row_ref, scratch
):
    place = place_ref[0]
    row_of = lax.broadcasted_iota(jnp.int32, (64, 256), 0)
    lane_of = lax.broadcasted_iota(jnp.int32, (128, 256), 0)
    lane = lax.broadcasted_iota(jnp.int32, (4, 128), 1)
    which = lax.broadcasted_iota(jnp.int32, (4, 128), 0)
    row = jnp.zeros((1, 128), F32)
    for j in range(4):
        row = jnp.where((lane[:1] & 3) == j, coupling_ref[j], row)
    row_ref[...] = row
    for slab in range(2):
        own = place == slab
        owners = []
        for slot in range(16):
            atom = jnp.where(own, own_ref[slot, 5:6, :128], other_ref[slot, 5:6, :128]).astype(jnp.int32)
            match = (lane == (8 * slab + atom) * 4 + which) & (atom >= 0)
            owners.append(jnp.where(match, 1.0, 0.0))
        table_ref[slab] = jnp.concatenate(owners + owners, axis=0)

        def one_slot(slot, carry, slab=slab, own=own):
            static = jnp.where(own, own_ref[slot], other_ref[slot])
            for k in range(4):
                piece = static[6 + k // 2 : 7 + k // 2, (k % 2) * 128 : (k % 2) * 128 + 128]
                potential_ref[slab * 64 + slot * 4 + k] = piece
            cell = static[4:5].astype(jnp.int32)
            at_row = jnp.where(row_of == (cell >> 7), 1.0, 0.0).astype(BF16)
            at_lane = jnp.where(lane_of == (cell & 127), 1.0, 0.0).astype(BF16)
            high, low = split(static[:4])
            found = []
            for part in (high, low):
                spread = jnp.concatenate([at_row * part[j : j + 1, :] for j in range(4)], axis=0)
                found.append(dot(spread, at_lane, NT))
            found = found[0] + found[1]
            for j in range(4):
                scratch[pl.ds(slot * 4 + j, 64, stride=64), :] = found[j * 64 : (j + 1) * 64]
            return carry

        lax.fori_loop(0, 16, one_slot, 0, unroll=4)

        def one_row(xy, carry, slab=slab):
            high, low = split(scratch[pl.ds(pl.multiple_of(xy * 64, 64), 64), :])
            dense_ref[slab * 64 + xy] = jnp.concatenate([high, low], axis=0)
            return carry

        lax.fori_loop(0, 64, one_row, 0, unroll=8)


def rows_of(refs, start, count):
    pieces = []
    for ref, low, high in zip(refs, (0, EDGE, ROWS - EDGE), (EDGE, ROWS - EDGE, ROWS)):
        first, end = max(start, low), min(start + count, high)
        if first < end:
            pieces.append(ref[first - low : end - low])
    return pieces[0] if len(pieces) == 1 else jnp.concatenate(pieces, axis=0)


def fetch(sources, targets, sems):
    copies = [
        pltpu.make_async_copy(source, target, sems.at[k])
        for k, (source, target) in enumerate(zip(sources, targets))
    ]
    for copy in copies:
        copy.start()
    for copy in copies:
        copy.wait()


def static_kernel(atom_hbm, potential_hbm, cell_hbm, proj_hbm, static_ref, *scratch):
    atom_ref, potential_ref, cell_ref, proj_ref, sems = scratch
    fetch((atom_hbm, potential_hbm, cell_hbm, proj_hbm), scratch[:4], sems)
    for slot in range(16):
        rows = potential_ref[slot * 4 : slot * 4 + 4]
        static_ref[slot] = jnp.concatenate(
            [
                proj_ref[slot],
                cell_ref[slot : slot + 1].astype(F32),
                jnp.full((1, 256), atom_ref[slot], jnp.int32).astype(F32),
                jnp.concatenate([rows[0:1], rows[1:2]], axis=1),
                jnp.concatenate([rows[2:3], rows[3:4]], axis=1),
            ],
            axis=0,
        )


def half_kernel(which_ref, orbitals_hbm, half_ref, orbitals_ref, sems):
    start = pl.multiple_of(which_ref[0] * (ORBS * 64), ORBS * 64)
    fetch((orbitals_hbm.at[pl.ds(start, ORBS * 64)],), (orbitals_ref,), sems)
    for xy in range(64):
        half_ref[xy] = orbitals_ref[pl.ds(xy, ORBS, stride=64), :]


def join_kernel(place_ref, odd_ref, own_ref, other_ref, left_ref, middle_ref, right_ref, *sends):
    for place in range(2):

        @pl.when(place_ref[0] == place)
        def _(place=place):
            first, second = (own_ref, other_ref) if place == 0 else (other_ref, own_ref)
            left_ref[...] = first[:EDGE]
            middle_ref[: 64 - EDGE] = first[EDGE:]
            middle_ref[64 - EDGE :] = second[: 64 - EDGE]
            right_ref[...] = second[64 - EDGE :]

    copy_faces(odd_ref, left_ref, right_ref, *sends)


def copy_faces(odd_ref, left_ref, right_ref, outer_ref, inner_ref):
    @pl.when(odd_ref[0] == 0)
    def _():
        outer_ref[...] = left_ref[...]
        inner_ref[...] = right_ref[...]

    @pl.when(odd_ref[0] == 1)
    def _():
        outer_ref[...] = right_ref[...]
        inner_ref[...] = left_ref[...]


def project(refs, dense_ref, table_ref):
    owner = jnp.zeros((ORBS, 128), F32)
    for slab in range(2):
        total = jnp.zeros((32, 128), F32)
        for xy in range(slab * 64, slab * 64 + 64, 2):
            pair = rows_of(refs, xy, 2)
            high, low = split(jnp.concatenate([pair[0], pair[1]], axis=1))
            dense = jnp.concatenate([dense_ref[xy], dense_ref[xy + 1]], axis=1)
            total = total + dot(jnp.concatenate([high, low], axis=0), dense, NT)
        owner = owner + exact_dot(total[:ORBS] + total[ORBS:], table_ref[slab])
    return owner


def project_kernel(left_ref, middle_ref, right_ref, dense_ref, table_ref, *outs):
    owner = project((left_ref, middle_ref, right_ref), dense_ref, table_ref)
    for out in outs:
        out[...] = owner


def local_kernel(alpha, center, with_previous, *refs):
    field, (potential_ref, matrix_ref) = refs[:3], refs[3:5]
    previous, out_ref = refs[5:8], refs[-1]
    scale = -0.5 * alpha
    along_y = (
        STENCIL[1] * scale,
        (STENCIL[2] + STENCIL[6]) * scale,
        (STENCIL[3] + STENCIL[5]) * scale,
        2.0 * STENCIL[4] * scale,
    )
    diagonal = alpha * (-1.5 * STENCIL[0] - center)
    for x in range(LAYERS):
        v = rows_of(field, x * NY, NY)
        flat = v.reshape(NY * ORBS, NZ)
        high, low = split(flat)
        product = dot(jnp.concatenate([high, low], axis=1), matrix_ref[...])
        total = (product[:, :NZ] + product[:, NZ:]).reshape(NY, ORBS, NZ)
        weight = potential_ref[x * NY : (x + 1) * NY] * alpha + diagonal
        total = total + weight * v
        for distance in range(1, 4):
            up = jnp.concatenate([v[distance:], v[:distance]], axis=0)
            down = jnp.concatenate([v[NY - distance :], v[: NY - distance]], axis=0)
            total = total + along_y[distance - 1] * (up + down)
        total = total + along_y[3] * jnp.concatenate([v[4:], v[:4]], axis=0)
        for distance in range(1, REACH + 1):
            near = None
            for at in (x - distance, x + distance):
                if 0 <= at < LAYERS:
                    piece = rows_of(field, at * NY, NY)
                    near = piece if near is None else near + piece
            if near is not None:
                total = total + (STENCIL[distance] * scale) * near
        if with_previous:
            total = total - rows_of(previous, x * NY, NY)
        out_ref[x * NY : (x + 1) * NY] = total


def spread_kernel(
    alpha, odd_ref, local_ref, own_ref, outer_ref, inner_ref, dense_ref, table_ref, coupling_ref, *outs
):
    lane = lax.broadcasted_iota(jnp.int32, (ORBS, 128), 1)
    left_lanes = jnp.where(odd_ref[0] == 0, 0, 64)
    outer, inner = (
        pltpu.roll(ref[...] if ref.ndim == 2 else ref[EDGE], 64, 1) for ref in (outer_ref, inner_ref)
    )
    total = own_ref[...] + jnp.where((lane & 64) == left_lanes, outer, inner)
    coefficient = total * (coupling_ref[...] * alpha)

    def write(row, value):
        for ref, low, high in zip(outs, (0, EDGE, ROWS - EDGE), (EDGE, ROWS - EDGE, ROWS)):
            if low <= row < high:
                ref[row - low] = value

    for slab in range(2):
        per_slot = exact_dot(coefficient, table_ref[slab], NT)
        weights = jnp.concatenate(split(per_slot), axis=0)
        for xy in range(slab * 64, slab * 64 + 64, 2):
            dense = jnp.concatenate([dense_ref[xy], dense_ref[xy + 1]], axis=1)
            term = dot(weights, dense)
            term = term[:ORBS] + term[ORBS:]
            write(xy, local_ref[xy] + term[:, :NZ])
            write(xy + 1, local_ref[xy + 1] + term[:, NZ:])


def faces(alpha, odd_ref, left_ref, right_ref, outer_ref, inner_ref, write_left, write_right):
    scale = -0.5 * alpha
    for odd in range(2):

        @pl.when(odd_ref[0] == odd)
        def _(odd=odd):
            from_left, from_right = (inner_ref, outer_ref) if odd else (outer_ref, inner_ref)
            for x in range(REACH):
                value = left_ref[x * NY : (x + 1) * NY]
                for distance in range(x + 1, REACH + 1):
                    at = (x - distance + REACH) * NY
                    value = value + (STENCIL[distance] * scale) * from_left[at : at + NY]
                write_left(odd, x, value)
                value = right_ref[x * NY : (x + 1) * NY]
                for distance in range(REACH - x, REACH + 1):
                    at = (x + distance - REACH) * NY
                    value = value + (STENCIL[distance] * scale) * from_right[at : at + NY]
                write_right(odd, x, value)


def faces_kernel(alpha, odd_ref, left_ref, right_ref, outer_ref, inner_ref, *outs):
    left_out, right_out, outer_out, inner_out = outs

    def write_left(odd, x, value):
        for ref in (left_out, inner_out if odd else outer_out):
            ref[x * NY : (x + 1) * NY] = value

    def write_right(odd, x, value):
        for ref in (right_out, outer_out if odd else inner_out):
            ref[x * NY : (x + 1) * NY] = value

    faces(alpha, odd_ref, left_ref, right_ref, outer_ref, inner_ref, write_left, write_right)


def whole_faces_kernel(
    alpha, with_sends, odd_ref, place_ref, member_ref, left_ref, middle_ref, right_ref, outer_ref, inner_ref, *rest
):
    if with_sends:
        (dense_ref, table_ref), rest = rest[:2], rest[2:]
    blocks, rest = rest[:4], rest[4:]
    if with_sends:
        whole_ref, return_ref, sums_ref, left_out, right_out, outer_out, inner_out = rest
    else:
        (whole_ref,) = rest

    def write_left(odd, x, value):
        whole_ref[x * NY : (x + 1) * NY] = value
        if with_sends:
            for ref in (left_out, inner_out if odd else outer_out):
                ref[x * NY : (x + 1) * NY] = value

    def write_right(odd, x, value):
        at = ROWS - EDGE + x * NY
        whole_ref[at : at + NY] = value
        if with_sends:
            for ref in (right_out, outer_out if odd else inner_out):
                ref[x * NY : (x + 1) * NY] = value

    faces(alpha, odd_ref, left_ref, right_ref, outer_ref, inner_ref, write_left, write_right)
    whole_ref[EDGE : ROWS - EDGE] = middle_ref[...]
    for step, ref in zip(STEPS, blocks):
        ref[...] = whole_ref[pl.ds(jnp.bitwise_xor(member_ref[0], step) * 32, 32)]
    if with_sends:
        owner = project((left_out, middle_ref, right_out), dense_ref, table_ref)
        sums_ref[...] = owner
        outer_out[EDGE] = owner
        inner_out[EDGE] = owner
        return_ref[...] = whole_ref[pl.ds((1 - place_ref[0]) * 64, 64)]


def gram(left, both_ref):
    total = jnp.zeros((128, 256), F32)
    for xy in range(0, 32, 2):
        piece = [jnp.concatenate([ref[xy], ref[xy + 1]], axis=1) for ref in left]
        rows = jnp.concatenate(split(jnp.concatenate(piece, axis=0)), axis=0)
        columns = jnp.concatenate([both_ref[xy], both_ref[xy + 1]], axis=1)
        total = total + dot(rows, columns, NT)
    total = total[:64] + total[64:]
    return total[:, :128] + total[:, 128:]


def field_gram_kernel(member_ref, core_ref, *refs):
    own, others, both_ref, margin_ref = refs[:4], refs[4:8], refs[8], refs[9]
    for k, step in enumerate(STEPS):
        member = jnp.bitwise_xor(member_ref[0], step)
        for ref, core in ((own[k], core_ref[0]), (others[k], 1 - core_ref[0])):
            band = jnp.bitwise_and(member, 1) * 2 + core
            at = pl.multiple_of(band * (2 * ORBS) + (member >> 1) * ORBS, ORBS)
            for xy in range(32):
                high, low = split(ref[xy])
                both_ref[xy, pl.ds(at, ORBS), :] = high
                both_ref[xy, pl.ds(128 + at, ORBS), :] = low
    margin_ref[...] = gram(own, both_ref)


def image_gram_kernel(member_ref, *refs):
    images, both_ref, margin_ref, out_ref = refs[:4], refs[4], refs[5], refs[6]
    total = gram(images, both_ref)
    for k, step in enumerate(STEPS):
        member = jnp.bitwise_xor(member_ref[0], step)
        out_ref[member, :ORBS] = margin_ref[k * ORBS : (k + 1) * ORBS]
        out_ref[member, ORBS:] = total[k * ORBS : (k + 1) * ORBS]


def copies_kernel(in_ref, out_ref):
    total = (in_ref[0] + in_ref[1]) + (in_ref[2] + in_ref[3])
    for copy in range(out_ref.shape[0]):
        out_ref[copy] = total


def sum_kernel(copies_ref, out_ref):
    parts = [copies_ref[copy] for copy in range(copies_ref.shape[0])]
    while len(parts) > 1:
        parts = [a + b for a, b in zip(parts[::2], parts[1::2])]
    out_ref[...] = parts[0]


def restore_kernel(place_ref, own_ref, other_ref, out_ref):
    place = place_ref[0]
    for orb in range(ORBS):
        for layer in range(8):
            at = layer * 8 * ORBS + orb
            mine = own_ref[pl.ds(place * (64 * ORBS) + at, 8, stride=ORBS), :]
            out_ref[place * ORBS + orb, layer] = mine
            out_ref[(1 - place) * ORBS + orb, layer] = other_ref[pl.ds(at, 8, stride=ORBS), :]


def along_z(alpha):
    circulant = np.zeros((NZ, NZ), np.float64)
    for row in range(NZ):
        for distance in range(1, REACH + 1):
            circulant[row, (row + distance) % NZ] += STENCIL[distance]
            circulant[row, (row - distance) % NZ] += STENCIL[distance]
    circulant = (circulant * (-0.5 * alpha)).astype(np.float32)
    high = circulant.astype(jnp.bfloat16)
    low = (circulant - high.astype(np.float32)).astype(jnp.bfloat16)
    return jnp.asarray(np.block([[high, low], [high, low]]))


def swap(value, axis, count, bit):
    return lax.ppermute(value, axis, [(i, i ^ bit) for i in range(count)])


def trade(blocks):
    return [swap(block, Y_RING, 4, step) if step else block for step, block in zip(STEPS, blocks)]


def meet(outer, inner, count):
    outer_pairs = [(i, (i + 1 if i % 2 else i - 1) % count) for i in range(count)]
    inner_pairs = [(i, i ^ 1) for i in range(count)]
    outer = lax.ppermute(outer, ("z", "x"), outer_pairs)
    return outer, lax.ppermute(inner, ("z", "x"), inner_pairs)


def in_order(place, own, other):
    return jnp.where(place == 0, jnp.stack([own, other]), jnp.stack([other, own]))


def shards(sizes, orbitals, potential, slot_atom, point_offset, projector, coupling):
    supers = sizes["z"] * sizes["x"]
    place = lax.axis_index("yl")
    place_1 = place.reshape(1).astype(jnp.int32)
    member_1 = lax.axis_index(Y_RING).reshape(1).astype(jnp.int32)
    core_1 = lax.axis_index("core").reshape(1).astype(jnp.int32)
    odd_1 = (lax.axis_index("x") % 2).reshape(1).astype(jnp.int32)
    block, half, field = (shape(rows, ORBS, NZ) for rows in (32, 64, ROWS))
    static = vmem_call(
        static_kernel,
        shape(16, 8, 256),
        (slot_atom, potential.reshape(64, NZ), point_offset, projector),
        scratch=(
            pltpu.SMEM((16,), jnp.int32),
            pltpu.VMEM((64, NZ), F32),
            pltpu.VMEM((16, 256), jnp.int32),
            pltpu.VMEM((16, 4, 256), F32),
            pltpu.SemaphoreType.DMA((4,)),
        ),
        flops=1 << 20,
        space=pltpu.HBM,
    )
    static, place_1, member_1, core_1, odd_1 = lax.optimization_barrier(
        (static, place_1, member_1, core_1, odd_1)
    )
    other_static = swap(static, "yl", 2, 1)

    def take(which):
        return vmem_call(
            half_kernel,
            half,
            (orbitals.reshape(2 * ORBS * 64, NZ),),
            scalars=(which,),
            scratch=(pltpu.VMEM((ORBS * 64, NZ), F32), pltpu.SemaphoreType.DMA((1,))),
            flops=1 << 20,
            space=pltpu.HBM,
        )

    outgoing, other_static = lax.optimization_barrier((take(1 - place_1), other_static))
    other_orbitals = swap(outgoing, "yl", 2, 1)
    own = take(place_1)
    dense, table, potential_rows, coupling_row = vmem_call(
        projector_kernel,
        [shape(ROWS, 128, NZ, dtype=BF16), shape(2, 128, 128), shape(ROWS, 1, NZ), shape(1, 128)],
        (static, other_static),
        scalars=(place_1, coupling),
        scratch=(pltpu.VMEM((64 * 64, NZ), F32),),
        flops=1 << 30,
    )
    face, middle = shape(EDGE, ORBS, NZ), shape(ROWS - 2 * EDGE, ORBS, NZ)
    three = [face, middle, face]
    dense, other_orbitals = lax.optimization_barrier((dense, other_orbitals))
    *current, outer, inner = vmem_call(
        join_kernel, three + [face, face], (own, other_orbitals), scalars=(place_1, odd_1), flops=1 << 20
    )
    previous = None
    for degree in range(5):
        last = degree == 4
        alpha = 1.0 if last else (2.0 if degree else 1.0) / HALF_WIDTH
        center = 0.0 if last else CENTER
        with_previous = degree > 0 and not last
        outer, inner = meet(outer, inner, supers)
        if last:
            fields = trade(blocks)
            outer_sums, inner_sums = outer, inner
        else:
            outer_sums, inner_sums = vmem_call(
                project_kernel, [shape(ORBS, 128)] * 2, (*current, dense, table), flops=1 << 29
            )
            sums = outer_sums
            outer_sums, inner_sums = meet(outer_sums, inner_sums, supers)
        local = vmem_call(
            functools.partial(local_kernel, alpha, center, with_previous),
            field,
            (*current, potential_rows, along_z(alpha)) + (tuple(previous) if with_previous else ()),
            flops=1 << 30,
        )
        left, center_rows, right = vmem_call(
            functools.partial(spread_kernel, alpha),
            three,
            (local, sums, outer_sums, inner_sums, dense, table, coupling_row),
            scalars=(odd_1,),
            flops=1 << 29,
        )
        if degree < 3:
            left, right, outer, inner = vmem_call(
                functools.partial(faces_kernel, alpha),
                [face] * 4,
                (left, right, outer, inner),
                scalars=(odd_1,),
                flops=1 << 24,
            )
            previous, current = current, [left, center_rows, right]
        elif degree == 3:
            message = shape(EDGE + 1, ORBS, NZ)
            *blocks, filtered, returning, sums, left, right, outer, inner = vmem_call(
                functools.partial(whole_faces_kernel, alpha, True),
                [block] * 4 + [field, half, shape(ORBS, 128)] + [face] * 2 + [message] * 2,
                (left, center_rows, right, outer, inner, dense, table),
                scalars=(odd_1, place_1, member_1),
                flops=1 << 24,
            )
            previous, current = current, [left, center_rows, right]
        else:
            left, center_rows, right, outer, inner, *fields = lax.optimization_barrier(
                (left, center_rows, right, outer, inner, *fields)
            )
            blocks = vmem_call(
                functools.partial(whole_faces_kernel, alpha, False),
                [block] * 4,
                (left, center_rows, right, outer, inner),
                scalars=(odd_1, place_1, member_1),
                scratch=(pltpu.VMEM((ROWS, ORBS, NZ), F32),),
                flops=1 << 24,
            )

    images = trade(blocks)
    others = [swap(value, "core", 2, 1) for value in fields]
    both, margins = vmem_call(
        field_gram_kernel,
        [shape(32, 256, NZ, dtype=BF16), shape(4 * ORBS, 128)],
        (*fields, *others),
        scalars=(member_1, core_1),
        flops=1 << 29,
    )
    products = vmem_call(
        image_gram_kernel,
        shape(4, 2 * ORBS, 128),
        (*images, both, margins),
        scalars=(member_1,),
        flops=1 << 29,
    )

    products = lax.all_to_all(products, Y_RING, 0, 0, tiled=True)

    returning, products = lax.optimization_barrier((returning, products))
    returned = swap(returning, "yl", 2, 1)
    restored = vmem_call(
        restore_kernel,
        shape(2 * ORBS, 8, NY, NZ),
        (filtered.reshape(ROWS * ORBS, NZ), returned.reshape(64 * ORBS, NZ)),
        scalars=(place_1,),
        flops=1 << 34,
    )

    copies = vmem_call(copies_kernel, shape(supers, 2 * ORBS, 128), (products,), flops=1 << 20)
    copies = lax.all_to_all(copies, ("z", "x"), 0, 0, tiled=True)
    total = vmem_call(sum_kernel, shape(2 * ORBS, 128), (copies,), flops=1 << 20)
    total = total.reshape(2, ORBS, 128)
    total, restored = lax.optimization_barrier((total, restored))
    total = in_order(place, total, swap(total, "yl", 2, 1))
    inverse_cells = 1.0 / (supers * LAYERS * NY * NZ)
    margin = (total[:, 0] * inverse_cells).reshape(2 * ORBS, 128).T
    projected = (total[:, 1] * inverse_cells).reshape(2 * ORBS, 128).T
    return restored, projected, margin


def solution(mesh):
    sizes = {"z": 8, "x": 4, "yl": 2, "yh": 2, "core": 2}
    fine = Mesh(mesh.devices.reshape(tuple(sizes.values())), tuple(sizes))
    dom, band = ("z", "x", "yl"), ("yh", "core")
    in_specs = (
        P(band, dom, None, None),
        P(dom, None, None),
        P(dom),
        P(dom, None),
        P(dom, None, None),
        P(),
    )
    out_specs = (P(band, dom, None, None), P(None, band), P(None, band))
    return jax.shard_map(
        functools.partial(shards, sizes),
        mesh=fine,
        in_specs=in_specs,
        out_specs=out_specs,
        check_vma=False,
    )
```

```python
import functools
import math

import jax
import jax.numpy as jnp
import numpy as np
from jax import lax
from jax.experimental import pallas as pl
from jax.experimental.pallas import tpu as pltpu
from jax.sharding import Mesh
from jax.sharding import PartitionSpec as P

STENCIL = (
    -5369.0 / 1800.0,
    12.0 / 7.0,
    -15.0 / 56.0,
    10.0 / 189.0,
    -1.0 / 112.0,
    2.0 / 1925.0,
    -1.0 / 16632.0,
)
CENTER = 9.0
HALF_WIDTH = 7.0
REACH = 6

LAYERS = 16
NY = 8
ORBS = 16
NZ = 128
ROWS = LAYERS * NY
EDGE = REACH * NY
F32 = jnp.float32
BF16 = jnp.bfloat16
NT = (((1,), (1,)), ((), ()))
NN = (((1,), (0,)), ((), ()))
Y_RING = ("yl", "yh")
STEPS = (0, 2, 3, 1)


def dot(a, b, dims=NN):
    return lax.dot_general(a, b, dims, preferred_element_type=F32)


def exact_dot(a, b, dims=NN):
    return lax.dot_general(
        a, b, dims, precision=lax.Precision.HIGHEST, preferred_element_type=F32
    )


def split(v):
    high = v.astype(BF16)
    return high, (v - high.astype(F32)).astype(BF16)


def vmem_call(kernel, out_shape, inputs, scalars=(), scratch=(), flops=0, space=pltpu.VMEM):
    many = isinstance(out_shape, (list, tuple))
    held = [*inputs, *(out_shape if many else [out_shape])]
    limit = (6 << 20) + sum(math.prod(v.shape) * v.dtype.itemsize for v in held)
    if space == pltpu.HBM:
        limit = 60 << 20
    specs = [pl.BlockSpec(memory_space=pltpu.SMEM)] * len(scalars)
    specs += [pl.BlockSpec(memory_space=space)] * len(inputs)
    out = pl.BlockSpec(memory_space=pltpu.VMEM)
    return pl.pallas_call(
        kernel,
        out_shape=out_shape,
        in_specs=specs,
        out_specs=[out] * len(out_shape) if many else out,
        scratch_shapes=list(scratch),
        compiler_params=pltpu.CompilerParams(vmem_limit_bytes=limit),
        cost_estimate=pl.CostEstimate(flops=flops, bytes_accessed=4 << 20, transcendentals=0),
    )(*scalars, *inputs)


def shape(*dims, dtype=F32):
    return jax.ShapeDtypeStruct(dims, dtype)


def projector_kernel(
    place_ref, coupling_ref, own_ref, other_ref, dense_ref, table_ref, potential_ref, row_ref, scratch
):
    place = place_ref[0]
    row_of = lax.broadcasted_iota(jnp.int32, (64, 256), 0)
    lane_of = lax.broadcasted_iota(jnp.int32, (128, 256), 0)
    lane = lax.broadcasted_iota(jnp.int32, (4, 128), 1)
    which = lax.broadcasted_iota(jnp.int32, (4, 128), 0)
    row = jnp.zeros((1, 128), F32)
    for j in range(4):
        row = jnp.where((lane[:1] & 3) == j, coupling_ref[j], row)
    row_ref[...] = row
    for slab in range(2):
        own = place == slab
        owners = []
        for slot in range(16):
            atom = jnp.where(own, own_ref[slot, 5:6, :128], other_ref[slot, 5:6, :128]).astype(jnp.int32)
            match = (lane == (8 * slab + atom) * 4 + which) & (atom >= 0)
            owners.append(jnp.where(match, 1.0, 0.0))
        table_ref[slab] = jnp.concatenate(owners + owners, axis=0)

        def one_slot(slot, carry, slab=slab, own=own):
            static = jnp.where(own, own_ref[slot], other_ref[slot])
            for k in range(4):
                piece = static[6 + k // 2 : 7 + k // 2, (k % 2) * 128 : (k % 2) * 128 + 128]
                potential_ref[slab * 64 + slot * 4 + k] = piece
            cell = static[4:5].astype(jnp.int32)
            at_row = jnp.where(row_of == (cell >> 7), 1.0, 0.0).astype(BF16)
            at_lane = jnp.where(lane_of == (cell & 127), 1.0, 0.0).astype(BF16)
            high, low = split(static[:4])
            found = []
            for part in (high, low):
                spread = jnp.concatenate([at_row * part[j : j + 1, :] for j in range(4)], axis=0)
                found.append(dot(spread, at_lane, NT))
            found = found[0] + found[1]
            for j in range(4):
                scratch[pl.ds(slot * 4 + j, 64, stride=64), :] = found[j * 64 : (j + 1) * 64]
            return carry

        lax.fori_loop(0, 16, one_slot, 0, unroll=4)

        def one_row(xy, carry, slab=slab):
            high, low = split(scratch[pl.ds(pl.multiple_of(xy * 64, 64), 64), :])
            dense_ref[slab * 64 + xy] = jnp.concatenate([high, low], axis=0)
            return carry

        lax.fori_loop(0, 64, one_row, 0, unroll=8)


def rows_of(refs, start, count):
    pieces = []
    for ref, low, high in zip(refs, (0, EDGE, ROWS - EDGE), (EDGE, ROWS - EDGE, ROWS)):
        first, end = max(start, low), min(start + count, high)
        if first < end:
            pieces.append(ref[first - low : end - low])
    return pieces[0] if len(pieces) == 1 else jnp.concatenate(pieces, axis=0)


def fetch(sources, targets, sems):
    copies = [
        pltpu.make_async_copy(source, target, sems.at[k])
        for k, (source, target) in enumerate(zip(sources, targets))
    ]
    for copy in copies:
        copy.start()
    for copy in copies:
        copy.wait()


def static_kernel(atom_hbm, potential_hbm, cell_hbm, proj_hbm, static_ref, *scratch):
    atom_ref, potential_ref, cell_ref, proj_ref, sems = scratch
    fetch((atom_hbm, potential_hbm, cell_hbm, proj_hbm), scratch[:4], sems)
    for slot in range(16):
        rows = potential_ref[slot * 4 : slot * 4 + 4]
        static_ref[slot] = jnp.concatenate(
            [
                proj_ref[slot],
                cell_ref[slot : slot + 1].astype(F32),
                jnp.full((1, 256), atom_ref[slot], jnp.int32).astype(F32),
                jnp.concatenate([rows[0:1], rows[1:2]], axis=1),
                jnp.concatenate([rows[2:3], rows[3:4]], axis=1),
            ],
            axis=0,
        )


def half_kernel(which_ref, orbitals_hbm, half_ref, orbitals_ref, sems):
    start = pl.multiple_of(which_ref[0] * (ORBS * 64), ORBS * 64)
    fetch((orbitals_hbm.at[pl.ds(start, ORBS * 64)],), (orbitals_ref,), sems)
    for xy in range(64):
        half_ref[xy] = orbitals_ref[pl.ds(xy, ORBS, stride=64), :]


def join_kernel(place_ref, odd_ref, own_ref, other_ref, left_ref, middle_ref, right_ref, *sends):
    for place in range(2):

        @pl.when(place_ref[0] == place)
        def _(place=place):
            first, second = (own_ref, other_ref) if place == 0 else (other_ref, own_ref)
            left_ref[...] = first[:EDGE]
            middle_ref[: 64 - EDGE] = first[EDGE:]
            middle_ref[64 - EDGE :] = second[: 64 - EDGE]
            right_ref[...] = second[64 - EDGE :]

    copy_faces(odd_ref, left_ref, right_ref, *sends)


def copy_faces(odd_ref, left_ref, right_ref, outer_ref, inner_ref):
    @pl.when(odd_ref[0] == 0)
    def _():
        outer_ref[...] = left_ref[...]
        inner_ref[...] = right_ref[...]

    @pl.when(odd_ref[0] == 1)
    def _():
        outer_ref[...] = right_ref[...]
        inner_ref[...] = left_ref[...]


def project(refs, dense_ref, table_ref):
    owner = jnp.zeros((ORBS, 128), F32)
    for slab in range(2):
        total = jnp.zeros((32, 128), F32)
        for xy in range(slab * 64, slab * 64 + 64, 2):
            pair = rows_of(refs, xy, 2)
            high, low = split(jnp.concatenate([pair[0], pair[1]], axis=1))
            dense = jnp.concatenate([dense_ref[xy], dense_ref[xy + 1]], axis=1)
            total = total + dot(jnp.concatenate([high, low], axis=0), dense, NT)
        owner = owner + exact_dot(total[:ORBS] + total[ORBS:], table_ref[slab])
    return owner


def project_kernel(left_ref, middle_ref, right_ref, dense_ref, table_ref, *outs):
    owner = project((left_ref, middle_ref, right_ref), dense_ref, table_ref)
    for out in outs:
        out[...] = owner


def local_kernel(alpha, center, with_previous, *refs):
    field, (potential_ref, matrix_ref) = refs[:3], refs[3:5]
    previous, out_ref = refs[5:8], refs[-1]
    scale = -0.5 * alpha
    along_y = (
        STENCIL[1] * scale,
        (STENCIL[2] + STENCIL[6]) * scale,
        (STENCIL[3] + STENCIL[5]) * scale,
        2.0 * STENCIL[4] * scale,
    )
    diagonal = alpha * (-1.5 * STENCIL[0] - center)
    for x in range(LAYERS):
        v = rows_of(field, x * NY, NY)
        flat = v.reshape(NY * ORBS, NZ)
        high, low = split(flat)
        product = dot(jnp.concatenate([high, low], axis=1), matrix_ref[...])
        total = (product[:, :NZ] + product[:, NZ:]).reshape(NY, ORBS, NZ)
        weight = potential_ref[x * NY : (x + 1) * NY] * alpha + diagonal
        total = total + weight * v
        for distance in range(1, 4):
            up = jnp.concatenate([v[distance:], v[:distance]], axis=0)
            down = jnp.concatenate([v[NY - distance :], v[: NY - distance]], axis=0)
            total = total + along_y[distance - 1] * (up + down)
        total = total + along_y[3] * jnp.concatenate([v[4:], v[:4]], axis=0)
        for distance in range(1, REACH + 1):
            near = None
            for at in (x - distance, x + distance):
                if 0 <= at < LAYERS:
                    piece = rows_of(field, at * NY, NY)
                    near = piece if near is None else near + piece
            if near is not None:
                total = total + (STENCIL[distance] * scale) * near
        if with_previous:
            total = total - rows_of(previous, x * NY, NY)
        out_ref[x * NY : (x + 1) * NY] = total


def spread_kernel(
    alpha, odd_ref, local_ref, own_ref, outer_ref, inner_ref, dense_ref, table_ref, coupling_ref, *outs
):
    lane = lax.broadcasted_iota(jnp.int32, (ORBS, 128), 1)
    left_lanes = jnp.where(odd_ref[0] == 0, 0, 64)
    outer, inner = (
        pltpu.roll(ref[...] if ref.ndim == 2 else ref[EDGE], 64, 1) for ref in (outer_ref, inner_ref)
    )
    total = own_ref[...] + jnp.where((lane & 64) == left_lanes, outer, inner)
    coefficient = total * (coupling_ref[...] * alpha)

    def write(row, value):
        for ref, low, high in zip(outs, (0, EDGE, ROWS - EDGE), (EDGE, ROWS - EDGE, ROWS)):
            if low <= row < high:
                ref[row - low] = value

    for slab in range(2):
        per_slot = exact_dot(coefficient, table_ref[slab], NT)
        weights = jnp.concatenate(split(per_slot), axis=0)
        for xy in range(slab * 64, slab * 64 + 64, 2):
            dense = jnp.concatenate([dense_ref[xy], dense_ref[xy + 1]], axis=1)
            term = dot(weights, dense)
            term = term[:ORBS] + term[ORBS:]
            write(xy, local_ref[xy] + term[:, :NZ])
            write(xy + 1, local_ref[xy + 1] + term[:, NZ:])


def faces(alpha, odd_ref, left_ref, right_ref, outer_ref, inner_ref, write_left, write_right):
    scale = -0.5 * alpha
    for odd in range(2):

        @pl.when(odd_ref[0] == odd)
        def _(odd=odd):
            from_left, from_right = (inner_ref, outer_ref) if odd else (outer_ref, inner_ref)
            for x in range(REACH):
                value = left_ref[x * NY : (x + 1) * NY]
                for distance in range(x + 1, REACH + 1):
                    at = (x - distance + REACH) * NY
                    value = value + (STENCIL[distance] * scale) * from_left[at : at + NY]
                write_left(odd, x, value)
                value = right_ref[x * NY : (x + 1) * NY]
                for distance in range(REACH - x, REACH + 1):
                    at = (x + distance - REACH) * NY
                    value = value + (STENCIL[distance] * scale) * from_right[at : at + NY]
                write_right(odd, x, value)


def faces_kernel(alpha, odd_ref, left_ref, right_ref, outer_ref, inner_ref, *outs):
    left_out, right_out, outer_out, inner_out = outs

    def write_left(odd, x, value):
        for ref in (left_out, inner_out if odd else outer_out):
            ref[x * NY : (x + 1) * NY] = value

    def write_right(odd, x, value):
        for ref in (right_out, outer_out if odd else inner_out):
            ref[x * NY : (x + 1) * NY] = value

    faces(alpha, odd_ref, left_ref, right_ref, outer_ref, inner_ref, write_left, write_right)


def whole_faces_kernel(
    alpha, with_sends, odd_ref, place_ref, member_ref, left_ref, middle_ref, right_ref, outer_ref, inner_ref, *rest
):
    if with_sends:
        (dense_ref, table_ref), rest = rest[:2], rest[2:]
    blocks, rest = rest[:4], rest[4:]
    if with_sends:
        whole_ref, return_ref, sums_ref, left_out, right_out, outer_out, inner_out = rest
    else:
        (whole_ref,) = rest

    def write_left(odd, x, value):
        whole_ref[x * NY : (x + 1) * NY] = value
        if with_sends:
            for ref in (left_out, inner_out if odd else outer_out):
                ref[x * NY : (x + 1) * NY] = value

    def write_right(odd, x, value):
        at = ROWS - EDGE + x * NY
        whole_ref[at : at + NY] = value
        if with_sends:
            for ref in (right_out, outer_out if odd else inner_out):
                ref[x * NY : (x + 1) * NY] = value

    faces(alpha, odd_ref, left_ref, right_ref, outer_ref, inner_ref, write_left, write_right)
    whole_ref[EDGE : ROWS - EDGE] = middle_ref[...]
    for step, ref in zip(STEPS, blocks):
        ref[...] = whole_ref[pl.ds(jnp.bitwise_xor(member_ref[0], step) * 32, 32)]
    if with_sends:
        owner = project((left_out, middle_ref, right_out), dense_ref, table_ref)
        sums_ref[...] = owner
        outer_out[EDGE] = owner
        inner_out[EDGE] = owner
        return_ref[...] = whole_ref[pl.ds((1 - place_ref[0]) * 64, 64)]


def gram(left, both_ref):
    total = jnp.zeros((128, 256), F32)
    for xy in range(0, 32, 2):
        piece = [jnp.concatenate([ref[xy], ref[xy + 1]], axis=1) for ref in left]
        rows = jnp.concatenate(split(jnp.concatenate(piece, axis=0)), axis=0)
        columns = jnp.concatenate([both_ref[xy], both_ref[xy + 1]], axis=1)
        total = total + dot(rows, columns, NT)
    total = total[:64] + total[64:]
    return total[:, :128] + total[:, 128:]


def field_gram_kernel(member_ref, core_ref, *refs):
    own, others, both_ref, margin_ref = refs[:4], refs[4:8], refs[8], refs[9]
    for k, step in enumerate(STEPS):
        member = jnp.bitwise_xor(member_ref[0], step)
        for ref, core in ((own[k], core_ref[0]), (others[k], 1 - core_ref[0])):
            band = jnp.bitwise_and(member, 1) * 2 + core
            at = pl.multiple_of(band * (2 * ORBS) + (member >> 1) * ORBS, ORBS)
            for xy in range(32):
                high, low = split(ref[xy])
                both_ref[xy, pl.ds(at, ORBS), :] = high
                both_ref[xy, pl.ds(128 + at, ORBS), :] = low
    margin_ref[...] = gram(own, both_ref)


def image_gram_kernel(*refs):
    images, both_ref, margin_ref, outs = refs[:4], refs[4], refs[5], refs[6:]
    total = gram(images, both_ref)
    for k, out in enumerate(outs):
        out[:ORBS] = margin_ref[k * ORBS : (k + 1) * ORBS]
        out[ORBS:] = total[k * ORBS : (k + 1) * ORBS]


def copies_kernel(a_ref, b_ref, c_ref, d_ref, out_ref):
    total = (a_ref[...] + b_ref[...]) + (c_ref[...] + d_ref[...])
    for copy in range(out_ref.shape[0]):
        out_ref[copy] = total


def sum_kernel(copies_ref, out_ref):
    parts = [copies_ref[copy] for copy in range(copies_ref.shape[0])]
    while len(parts) > 1:
        parts = [a + b for a, b in zip(parts[::2], parts[1::2])]
    out_ref[...] = parts[0]


def restore_kernel(place_ref, own_ref, other_ref, out_ref):
    place = place_ref[0]
    for orb in range(ORBS):
        for layer in range(8):
            at = layer * 8 * ORBS + orb
            mine = own_ref[pl.ds(place * (64 * ORBS) + at, 8, stride=ORBS), :]
            out_ref[place * ORBS + orb, layer] = mine
            out_ref[(1 - place) * ORBS + orb, layer] = other_ref[pl.ds(at, 8, stride=ORBS), :]


def along_z(alpha):
    circulant = np.zeros((NZ, NZ), np.float64)
    for row in range(NZ):
        for distance in range(1, REACH + 1):
            circulant[row, (row + distance) % NZ] += STENCIL[distance]
            circulant[row, (row - distance) % NZ] += STENCIL[distance]
    circulant = (circulant * (-0.5 * alpha)).astype(np.float32)
    high = circulant.astype(jnp.bfloat16)
    low = (circulant - high.astype(np.float32)).astype(jnp.bfloat16)
    return jnp.asarray(np.block([[high, low], [high, low]]))


def swap(value, axis, count, bit):
    return lax.ppermute(value, axis, [(i, i ^ bit) for i in range(count)])


def trade(blocks):
    return [swap(block, Y_RING, 4, step) if step else block for step, block in zip(STEPS, blocks)]


def meet(outer, inner, count):
    outer_pairs = [(i, (i + 1 if i % 2 else i - 1) % count) for i in range(count)]
    inner_pairs = [(i, i ^ 1) for i in range(count)]
    outer = lax.ppermute(outer, ("z", "x"), outer_pairs)
    return outer, lax.ppermute(inner, ("z", "x"), inner_pairs)


def in_order(place, own, other):
    return jnp.where(place == 0, jnp.stack([own, other]), jnp.stack([other, own]))


def shards(sizes, orbitals, potential, slot_atom, point_offset, projector, coupling):
    supers = sizes["z"] * sizes["x"]
    place = lax.axis_index("yl")
    place_1 = place.reshape(1).astype(jnp.int32)
    member_1 = lax.axis_index(Y_RING).reshape(1).astype(jnp.int32)
    core_1 = lax.axis_index("core").reshape(1).astype(jnp.int32)
    odd_1 = (lax.axis_index("x") % 2).reshape(1).astype(jnp.int32)
    block, half, field = (shape(rows, ORBS, NZ) for rows in (32, 64, ROWS))
    static = vmem_call(
        static_kernel,
        shape(16, 8, 256),
        (slot_atom, potential.reshape(64, NZ), point_offset, projector),
        scratch=(
            pltpu.SMEM((16,), jnp.int32),
            pltpu.VMEM((64, NZ), F32),
            pltpu.VMEM((16, 256), jnp.int32),
            pltpu.VMEM((16, 4, 256), F32),
            pltpu.SemaphoreType.DMA((4,)),
        ),
        flops=1 << 20,
        space=pltpu.HBM,
    )
    static, place_1, member_1, core_1, odd_1 = lax.optimization_barrier(
        (static, place_1, member_1, core_1, odd_1)
    )
    other_static = swap(static, "yl", 2, 1)

    def take(which):
        return vmem_call(
            half_kernel,
            half,
            (orbitals.reshape(2 * ORBS * 64, NZ),),
            scalars=(which,),
            scratch=(pltpu.VMEM((ORBS * 64, NZ), F32), pltpu.SemaphoreType.DMA((1,))),
            flops=1 << 20,
            space=pltpu.HBM,
        )

    outgoing, other_static = lax.optimization_barrier((take(1 - place_1), other_static))
    other_orbitals = swap(outgoing, "yl", 2, 1)
    own = take(place_1)
    dense, table, potential_rows, coupling_row = vmem_call(
        projector_kernel,
        [shape(ROWS, 128, NZ, dtype=BF16), shape(2, 128, 128), shape(ROWS, 1, NZ), shape(1, 128)],
        (static, other_static),
        scalars=(place_1, coupling),
        scratch=(pltpu.VMEM((64 * 64, NZ), F32),),
        flops=1 << 30,
    )
    face, middle = shape(EDGE, ORBS, NZ), shape(ROWS - 2 * EDGE, ORBS, NZ)
    three = [face, middle, face]
    dense, other_orbitals = lax.optimization_barrier((dense, other_orbitals))
    *current, outer, inner = vmem_call(
        join_kernel, three + [face, face], (own, other_orbitals), scalars=(place_1, odd_1), flops=1 << 20
    )
    previous = None
    for degree in range(5):
        last = degree == 4
        alpha = 1.0 if last else (2.0 if degree else 1.0) / HALF_WIDTH
        center = 0.0 if last else CENTER
        with_previous = degree > 0 and not last
        outer, inner = meet(outer, inner, supers)
        if last:
            fields = trade(blocks)
            outer_sums, inner_sums = outer, inner
        else:
            outer_sums, inner_sums = vmem_call(
                project_kernel, [shape(ORBS, 128)] * 2, (*current, dense, table), flops=1 << 29
            )
            sums = outer_sums
            outer_sums, inner_sums = meet(outer_sums, inner_sums, supers)
        local = vmem_call(
            functools.partial(local_kernel, alpha, center, with_previous),
            field,
            (*current, potential_rows, along_z(alpha)) + (tuple(previous) if with_previous else ()),
            flops=1 << 30,
        )
        left, center_rows, right = vmem_call(
            functools.partial(spread_kernel, alpha),
            three,
            (local, sums, outer_sums, inner_sums, dense, table, coupling_row),
            scalars=(odd_1,),
            flops=1 << 29,
        )
        if degree < 3:
            left, right, outer, inner = vmem_call(
                functools.partial(faces_kernel, alpha),
                [face] * 4,
                (left, right, outer, inner),
                scalars=(odd_1,),
                flops=1 << 24,
            )
            previous, current = current, [left, center_rows, right]
        elif degree == 3:
            message = shape(EDGE + 1, ORBS, NZ)
            *blocks, filtered, returning, sums, left, right, outer, inner = vmem_call(
                functools.partial(whole_faces_kernel, alpha, True),
                [block] * 4 + [field, half, shape(ORBS, 128)] + [face] * 2 + [message] * 2,
                (left, center_rows, right, outer, inner, dense, table),
                scalars=(odd_1, place_1, member_1),
                flops=1 << 24,
            )
            previous, current = current, [left, center_rows, right]
        else:
            blocks = vmem_call(
                functools.partial(whole_faces_kernel, alpha, False),
                [block] * 4,
                (left, center_rows, right, outer, inner),
                scalars=(odd_1, place_1, member_1),
                scratch=(pltpu.VMEM((ROWS, ORBS, NZ), F32),),
                flops=1 << 24,
            )

    both = lax.optimization_barrier((*fields, *blocks))
    fields, blocks = both[:4], both[4:]
    images = trade(blocks)
    others = [swap(value, "core", 2, 1) for value in fields]
    both, margins = vmem_call(
        field_gram_kernel,
        [shape(32, 256, NZ, dtype=BF16), shape(4 * ORBS, 128)],
        (*fields, *others),
        scalars=(member_1, core_1),
        flops=1 << 29,
    )
    products = vmem_call(
        image_gram_kernel, [shape(2 * ORBS, 128)] * 4, (*images, both, margins), flops=1 << 29
    )
    products = trade(products)

    returning, *products = lax.optimization_barrier((returning, *products))
    returned = swap(returning, "yl", 2, 1)
    restored = vmem_call(
        restore_kernel,
        shape(2 * ORBS, 8, NY, NZ),
        (filtered.reshape(ROWS * ORBS, NZ), returned.reshape(64 * ORBS, NZ)),
        scalars=(place_1,),
        flops=1 << 34,
    )

    copies = vmem_call(copies_kernel, shape(supers, 2 * ORBS, 128), tuple(products), flops=1 << 20)
    copies = lax.all_to_all(copies, ("z", "x"), 0, 0, tiled=True)
    total = vmem_call(sum_kernel, shape(2 * ORBS, 128), (copies,), flops=1 << 20)
    total = total.reshape(2, ORBS, 128)
    total, restored = lax.optimization_barrier((total, restored))
    total = in_order(place, total, swap(total, "yl", 2, 1))
    inverse_cells = 1.0 / (supers * LAYERS * NY * NZ)
    margin = (total[:, 0] * inverse_cells).reshape(2 * ORBS, 128).T
    projected = (total[:, 1] * inverse_cells).reshape(2 * ORBS, 128).T
    return restored, projected, margin


def solution(mesh):
    sizes = {"z": 8, "x": 4, "yl": 2, "yh": 2, "core": 2}
    fine = Mesh(mesh.devices.reshape(tuple(sizes.values())), tuple(sizes))
    dom, band = ("z", "x", "yl"), ("yh", "core")
    in_specs = (
        P(band, dom, None, None),
        P(dom, None, None),
        P(dom),
        P(dom, None),
        P(dom, None, None),
        P(),
    )
    out_specs = (P(band, dom, None, None), P(None, band), P(None, band))
    return jax.shard_map(
        functools.partial(shards, sizes),
        mesh=fine,
        in_specs=in_specs,
        out_specs=out_specs,
        check_vma=False,
    )
```
